256 devices in a mesh: expert: 64 (over z, x, core), inner: 4 (over y).
Axes of the slice: x: 4, y: 4, z: 8, core: 2. Of those that a mesh axis runs over, the one named last changes fastest.
Arguments:
- tokens_one: bfloat16 [1024, 7168], P('expert', 'inner'), may hold values from -6 to 6
- experts_one: int32 [1024, 8], P('expert'), may hold values from 0 to 63, as said below
- gates_one: float32 [1024, 8], P('expert'), may hold values from 0.1 to 1
- tokens_two: bfloat16 [1024, 7168], P('expert', 'inner'), may hold values from -6 to 6
- experts_two: int32 [1024, 8], P('expert'), may hold values from 0 to 63, as said below
- gates_two: float32 [1024, 8], P('expert'), may hold values from 0.1 to 1
- replica_pick: int32 [1024, 8], P('expert'), may hold values from 0 to 839
- home: int32 [64], replicated, may hold values from 0 to 63, each once
- w_gate_up: bfloat16 [64, 2, 7168, 1024], P('expert', None, None, 'inner'), may hold values from -0.0625 to 0.0625
- w_down: bfloat16 [64, 1024, 7168], P('expert', 'inner'), may hold values from -0.1875 to 0.1875
Outputs:
- mixed_one: bfloat16 [1024, 7168], P('expert', 'inner')
- mixed_two: bfloat16 [1024, 7168], P('expert', 'inner')
The draws below stay inside these ranges and needn't reach their ends.
Inputs may be any that keep to these rules, and one draw needn't show every extreme that they name: `experts_one`: each row names 8 different experts. `experts_two`: each row names 8 different experts.
All inputs are finite; a program needn't handle non-finite values.
Results may differ from the reference program's by a relative error of at most 0.0058.
Values may be sent and summed in bfloat16 or wider, within the bound.
A program may use at most 128 MiB of HBM per device.

```python
import math
import jax
import jax.numpy as jnp
from jax import lax

D = 7168
FF = 1024
TOPK = 8
COPIES = 3
TOK_DEV = 16
SPECIALIST_TOTAL = 64
TOKENS = 1024
SLOT = 2


def choose_experts(own_key, shared_seed):
    ranking = jax.random.permutation(shared_seed, SPECIALIST_TOTAL)
    source = jnp.arange(TOKENS, dtype=jnp.int32) // TOK_DEV
    upper_half = (source * 2 >= SPECIALIST_TOTAL)[:, None]
    lower_part = (source * 8 < 3 * SPECIALIST_TOTAL)[:, None]
    first_fav = (ranking == 0)[None, :]
    second_fav = (ranking == 1)[None, :]
    logit_uplift = jnp.where(upper_half & first_fav, 2097152, 0) + jnp.where(lower_part & second_fav, 2097152, 0)
    jitter_sample = jax.random.randint(own_key, (TOKENS, SPECIALIST_TOTAL), 0, 1048576, dtype=jnp.int32)
    gating_logits = (jitter_sample + logit_uplift.astype(jnp.int32)) * SPECIALIST_TOTAL + jnp.arange(SPECIALIST_TOTAL, dtype=jnp.int32)[None, :]
    best_scores, picked = lax.top_k(gating_logits, TOPK)
    return picked.astype(jnp.int32)


def draw_experts_one(key, part):
    shared_seed = key
    key = jax.random.fold_in(key, 11)
    return choose_experts(key, shared_seed)


def draw_experts_two(key, part):
    shared_seed = key
    key = jax.random.fold_in(key, 23)
    return choose_experts(key, shared_seed)


def place_ends(drawn, key, smallest, top_value):
    longest = drawn.shape.index(max(drawn.shape))
    spots = []
    for shift in (0, 1):
        where = [jax.random.randint(jax.random.fold_in(key, axis), (), 0, length) for axis, length in enumerate(drawn.shape)]
        where[longest] = (where[longest] + shift) % drawn.shape[longest]
        spots.append(tuple(where))
    return drawn.at[spots[0]].set(smallest).at[spots[1]].set(top_value)


def steps_of(stream_key, extent, pieces, low, high):
    factor_of, own = 1.0, jax.random.fold_in(stream_key, 6)
    for position, parts in pieces:
        draws = jnp.exp(jax.random.uniform(jax.random.fold_in(own, position), (parts,), jnp.float32, low / len(pieces), high / len(pieces)))
        factor_of = factor_of * jnp.repeat(draws, extent[position] // parts).reshape([-1 if axis == position else 1 for axis in range(len(extent))])
    return factor_of


def noise(stream_key, dims, spread, most, cuts=(), kind=jnp.bfloat16):
    result = jax.random.normal(stream_key, dims, jnp.float32) * spread
    if len(cuts) > 0:
        result = steps_of(stream_key, dims, cuts, -0.22, 0.18) * result
    return jnp.clip(result, min=-most, max=most).astype(kind)


def setup_inputs(seed: int = 0) -> dict:
    streams_of = jax.random.split(jax.random.key(seed), 11)
    return {
        "tokens_one": noise(streams_of[0], (TOKENS, D), 1.0, 6.0, ((0, 64), (1, 4))),
        "experts_one": draw_experts_one(jax.random.fold_in(streams_of[10], 71), 0),
        "gates_one": jnp.clip(jnp.exp(math.log(1.0) - 2.3025851 * jax.random.uniform(streams_of[2], (TOKENS, TOPK), jnp.float32) ** steps_of(streams_of[2], (TOKENS, TOPK), ((0, 64),), -0.2, 0.2)), 0.1, 1.0),
        "tokens_two": noise(streams_of[3], (TOKENS, D), 1.0, 6.0, ((0, 64), (1, 4))),
        "experts_two": draw_experts_two(jax.random.fold_in(streams_of[10], 71), 0),
        "gates_two": jnp.clip(jnp.exp(math.log(1.0) - 2.3025851 * jax.random.uniform(streams_of[5], (TOKENS, TOPK), jnp.float32) ** steps_of(streams_of[5], (TOKENS, TOPK), ((0, 64),), -0.2, 0.2)), 0.1, 1.0),
        "replica_pick": place_ends(jax.random.randint(streams_of[6], (TOKENS, TOPK), 0, 840), jax.random.fold_in(streams_of[6], 1), 0, 839).astype(jnp.int32),
        "home": jax.random.permutation(streams_of[7], SPECIALIST_TOTAL).astype(jnp.int32),
        "w_gate_up": noise(streams_of[8], (SPECIALIST_TOTAL, 2, D, FF), D ** -0.5, 0.0625, ((0, 64), (3, 4))),
        "w_down": noise(streams_of[9], (SPECIALIST_TOTAL, FF, D), FF ** -0.5, 0.1875, ((0, 64), (1, 4))),
    }


def tally_counts(length):
    return jnp.arange(length, dtype=jnp.int32)


def table_lookup(lookup_table, positions):
    matches = positions[..., None] == tally_counts(lookup_table.shape[0])
    return jnp.sum(jnp.where(matches, lookup_table, 0), axis=-1, dtype=jnp.int32)


def rank_within(keys, key_count):
    onehot = (keys[..., None] == tally_counts(key_count)).astype(jnp.int32)
    running = jnp.cumsum(onehot, axis=-2, dtype=jnp.int32)
    return jnp.sum(running * onehot, axis=-1, dtype=jnp.int32) - 1


def layout_from_demand(counts, home):
    experts = home.shape[0]
    hot_expert = jnp.argmax(counts).astype(jnp.int32)
    busiest_resident = table_lookup(home, hot_expert)
    numbers = tally_counts(COPIES) + 1
    offsets = (numbers // 2) * (experts // 2) + numbers % 2
    copies = (busiest_resident + offsets) % experts
    return hot_expert, busiest_resident, copies.astype(jnp.int32)


def destinations(chosen, replica_pick, home, hot_expert, copies, second):
    owner_dev = table_lookup(home, chosen)
    if not second:
        zeros_like = jnp.zeros_like(owner_dev)
        return owner_dev, zeros_like, owner_dev, zeros_like
    replica_number = replica_pick % (COPIES + 1)
    to_copy = (chosen == hot_expert) & (replica_number > 0)
    target = table_lookup(copies, replica_number - 1)
    replica_dev = jnp.where(to_copy, target, owner_dev).astype(jnp.int32)
    return replica_dev, to_copy.astype(jnp.int32), owner_dev, replica_number


def expert_rows(gathered, weight_in, weight_out):
    gate = jnp.dot(gathered, weight_in[0], preferred_element_type=jnp.float32)
    up_part = jnp.dot(gathered, weight_in[1], preferred_element_type=jnp.float32)
    active = (jax.nn.silu(gate) * up_part).astype(jnp.bfloat16)
    return jnp.dot(active, weight_out, preferred_element_type=jnp.float32).astype(jnp.bfloat16)


def one_batch(tokens, chosen, gates, replica_pick, home, w_gate_up, w_down, hot_expert, busiest_resident, copies, second):
    devices = home.shape[0]
    replica_dev, replica_slot, owner_dev, replica_number = destinations(chosen, replica_pick, home, hot_expert, copies, second)
    keys = (replica_dev * 2 + replica_slot).reshape(devices, -1)
    slot_rank = rank_within(keys, 2 * devices)
    is_kept = slot_rank < SLOT
    source = tally_counts(devices)[:, None]
    slot_block = jnp.where(replica_slot.reshape(devices, -1) > 0, devices + replica_number.reshape(devices, -1) - 1, replica_dev.reshape(devices, -1))
    total_len = (devices + COPIES) * devices * SLOT
    where_to = (slot_block * devices + source) * SLOT + slot_rank
    where_to = jnp.where(is_kept, where_to, total_len).reshape(-1).astype(jnp.int32)
    token_owner = tally_counts(where_to.shape[0]) // TOPK
    source_row = jnp.zeros((total_len + 1,), jnp.int32).at[where_to].set(token_owner)
    filled = jnp.zeros((total_len + 1,), jnp.bool_).at[where_to].set(True)
    gathered = jnp.where(filled[:total_len, None], tokens[source_row[:total_len]], jnp.zeros((), jnp.bfloat16))
    gathered = gathered.reshape(devices + COPIES, devices * SLOT, tokens.shape[1])
    weight_index = jnp.concatenate([tally_counts(devices), jnp.zeros((COPIES,), jnp.int32) + busiest_resident])

    def per_block(pair):
        block_rows, index_now = pair
        weight_in = lax.dynamic_index_in_dim(w_gate_up, index_now, 0, keepdims=False)
        weight_out = lax.dynamic_index_in_dim(w_down, index_now, 0, keepdims=False)
        return expert_rows(block_rows, weight_in, weight_out)

    expert_out = lax.map(per_block, (gathered, weight_index))
    flat_rows = expert_out.reshape(total_len, tokens.shape[1])
    flat_rows = jnp.concatenate([flat_rows, jnp.zeros((1, tokens.shape[1]), jnp.bfloat16)], axis=0)
    picked = flat_rows[where_to].astype(jnp.float32)
    weighted = gates.reshape(-1)[:, None] * picked
    return jnp.sum(weighted.reshape(tokens.shape[0], TOPK, -1), axis=1).astype(jnp.bfloat16)


def reference(tokens_one, experts_one, gates_one, tokens_two, experts_two, gates_two, replica_pick, home, w_gate_up, w_down):
    experts = home.shape[0]
    counts = jnp.sum((experts_one.reshape(-1)[:, None] == tally_counts(experts)[None, :]).astype(jnp.int32), axis=0, dtype=jnp.int32)
    hot_expert, busiest_resident, copies = layout_from_demand(counts, home)
    mixed_one = one_batch(tokens_one, experts_one, gates_one, replica_pick, home, w_gate_up, w_down, hot_expert, busiest_resident, copies, False)
    mixed_two = one_batch(tokens_two, experts_two, gates_two, replica_pick, home, w_gate_up, w_down, hot_expert, busiest_resident, copies, True)
    return mixed_one, mixed_two
```

```python
import functools

import jax
import jax.numpy as jnp
from jax import lax
from jax.experimental import pallas as pl
from jax.experimental.pallas import tpu as pltpu
from jax.sharding import PartitionSpec as P

MESH = pl.DeviceIdType.MESH
TOPK = 8
COPIES = 3
SLOT = 2
CORES = 2
F32 = jnp.float32
BF16 = jnp.bfloat16
E1, G1, E2, G2, PICK = 0, 8, 16, 24, 32


def dot(a, b):
    return jnp.dot(a, b, preferred_element_type=F32)


def iota(shape, dim):
    return lax.broadcasted_iota(jnp.int32, shape, dim)


class Copies:
    def __init__(self, n, me, src, dst, device, send, recv):
        self.items = []
        for i in range(1, n):
            peer = lax.rem(me + i, n)
            self.items.append(
                pltpu.make_async_remote_copy(
                    src_ref=src(peer),
                    dst_ref=dst(me),
                    send_sem=send.at[i],
                    recv_sem=recv.at[i],
                    device_id=device(peer),
                    device_id_type=MESH,
                )
            )

    def start(self):
        for item in self.items:
            item.start()

    def wait_recv(self):
        for item in self.items:
            item.wait_recv()

    def wait_send(self):
        for item in self.items:
            item.wait_send()


class Ring:
    def __init__(self, n, me, block, half, device, send, recv):
        self.steps = n // 2
        self.pairs = []
        right, left = lax.rem(me + 1, n), lax.rem(me + n - 1, n)
        for k in range(1, self.steps + 1):
            pair = []
            for way, (target, index) in enumerate(
                ((right, lax.rem(me + n - (k - 1), n)), (left, lax.rem(me + (k - 1), n)))
            ):
                ref = half(index, way) if k == self.steps else block(index)
                pair.append(
                    pltpu.make_async_remote_copy(
                        src_ref=ref,
                        dst_ref=ref,
                        send_sem=send.at[2 * k + way],
                        recv_sem=recv.at[2 * k + way],
                        device_id=device(target),
                        device_id_type=MESH,
                    )
                )
            self.pairs.append(pair)

    def start(self, k):
        for item in self.pairs[k - 1]:
            item.start()

    def wait_recv(self, k):
        for item in self.pairs[k - 1]:
            item.wait_recv()

    def wait_send(self):
        for pair in self.pairs:
            for item in pair:
                item.wait_send()


def kernel(
    dims,
    tok1,
    tok2,
    info_in,
    home,
    w_in,
    w_out,
    out1,
    out2,
    z1,
    z2,
    info,
    counts,
    xs1,
    y1,
    xs2,
    xr2,
    hid1,
    hid2,
    wgu,
    wd,
    acc,
    o1,
    o2,
    ro1,
    ro2,
    mix1,
    mix2,
    mr1,
    mr2,
    local,
    *sems,
):
    nz, nx, ny = dims
    npl = nx * CORES
    tok = tok1.shape[0]
    feat = tok1.shape[1]
    width = feat * ny
    ff = w_in.shape[3]
    cols = nz * tok
    s1 = SLOT * nz
    s2 = (COPIES + 1) * s1
    sems = list(sems)

    e = lax.axis_index("expert")
    y = lax.axis_index("inner")
    z = e // npl
    p = lax.rem(e, npl)
    x = p // CORES
    c = lax.rem(p, CORES)
    zdev = lambda other: (other * npl + p, y)
    pdev = lambda other: (z * npl + other, y)
    ydev = lambda other: (e, other)
    xdev = lambda other: (z * npl + other * CORES + c, y)

    def pair():
        return sems.pop(0), sems.pop(0)

    def rows(ref, start, size):
        return ref.at[pl.ds(start, size)]

    def lanes(ref, index, size):
        return ref.at[:, pl.ds(pl.multiple_of(index * size, size), size)]

    def block(ref, r, rs, l, ls):
        return ref.at[pl.ds(r, rs), pl.ds(pl.multiple_of(l, ls), ls)]

    weights = pltpu.make_async_copy(w_in.at[0], wgu, local.at[0])
    weights.start()
    own_out = pltpu.make_async_copy(
        lanes(w_out.at[0], y, feat), rows(wd, y * ff, ff), local.at[1]
    )
    own_out.start()

    barrier = pltpu.get_barrier_semaphore()
    for i in range(1, nz):
        pl.semaphore_signal(barrier, inc=1, device_id=zdev(lax.rem(z + i, nz)), device_id_type=MESH)
    for i in range(1, npl):
        pl.semaphore_signal(barrier, inc=1, device_id=pdev(lax.rem(p + i, npl)), device_id_type=MESH)
    for i in range(1, ny):
        pl.semaphore_signal(barrier, inc=1, device_id=ydev(lax.rem(y + i, ny)), device_id_type=MESH)
    pl.semaphore_wait(barrier, nz + npl + ny - 3)

    started = []

    def go(copies):
        copies.start()
        started.append(copies)
        return copies

    info_z = go(Copies(nz, z, lambda o: info_in, lambda m: rows(info, m * tok, tok), zdev, *pair()))
    tok2_y = go(Copies(ny, y, lambda o: tok2, lambda m: lanes(rows(z2, z * tok, tok), m, feat), ydev, *pair()))
    tok1_z = go(Copies(nz, z, lambda o: tok1, lambda m: rows(z1, m * tok, tok), zdev, *pair()))
    info[pl.ds(z * tok, tok), :] = info_in[...]
    z1[pl.ds(z * tok, tok), :] = tok1[...]
    z2[pl.ds(z * tok, tok), pl.ds(pl.multiple_of(y * feat, feat), feat)] = tok2[...]
    tok2_y.wait_recv()
    ring2 = Ring(
        nz,
        z,
        lambda i: rows(z2, i * tok, tok),
        lambda i, h: block(z2, i * tok, tok, h * (width // 2), width // 2),
        zdev,
        *pair(),
    )
    ring2.start(1)
    out_y = go(
        Copies(
            ny, y, lambda o: lanes(w_out.at[0], o, feat), lambda m: rows(wd, m * ff, ff), ydev, *pair()
        )
    )

    info_z.wait_recv()
    every = info[...]
    turned = every.T
    field = lambda base, k: turned[base + k : base + k + 1, :]
    expert_lane = iota((cols, 128), 1).astype(F32)
    tally = jnp.zeros((cols, 128), F32)
    for k in range(TOPK):
        tally += (every[:, E1 + k : E1 + k + 1] == expert_lane).astype(F32)
    own_counts = jnp.broadcast_to(jnp.sum(tally, axis=0, keepdims=True), (8, 128))
    counts[pl.ds(p * 8, 8), :] = own_counts
    counts_p = go(
        Copies(npl, p, lambda o: rows(counts, p * 8, 8), lambda m: rows(counts, m * 8, 8), pdev, *pair())
    )

    shape = (cols, cols)
    earlier = ((iota(shape, 0) // tok == iota(shape, 1) // tok) & (iota(shape, 0) < iota(shape, 1))).astype(BF16)

    def resident(length, per):
        target = z * npl + iota((length, 128), 0) // per
        holds = home[0:1, :] == target
        lane = iota((length, 128), 1).astype(F32)
        return jnp.sum(jnp.where(holds, lane, 0.0), axis=1, keepdims=True)

    def selection(match, length):
        number = dot(match.astype(BF16), earlier)
        slot = (iota((length, cols), 0) // nz % SLOT).astype(F32)
        return jnp.where(number == slot, match, 0.0)

    n1 = npl * s1
    same_z = (iota((n1, cols), 0) % nz) == (iota((n1, cols), 1) // tok)
    holder = resident(n1, s1)
    match = jnp.zeros((n1, cols), F32)
    gate = jnp.zeros((n1, cols), F32)
    for k in range(TOPK):
        hit = (field(E1, k) == holder) & same_z
        match += hit.astype(F32)
        gate += jnp.where(hit, field(G1, k), 0.0)
    sel1 = selection(match, n1)
    mixer1 = (sel1 * gate).T

    tok1_z.wait_recv()
    xs1[...] = dot(sel1.astype(BF16), z1[...]).astype(BF16)
    mine = lambda ref: lanes(ref, y, feat)
    x1 = go(
        Copies(
            npl, p, lambda o: rows(xs1, o * s1, s1), lambda m: mine(rows(y1, m * s1, s1)), pdev, *pair()
        )
    )
    y1[pl.ds(p * s1, s1), pl.ds(pl.multiple_of(y * feat, feat), feat)] = xs1[pl.ds(p * s1, s1), :]

    counts_p.wait_recv()
    total = counts[0:8, :]
    for other in range(1, npl):
        total += counts[other * 8 : other * 8 + 8, :]
    total = total[0:1, :]
    lane = iota((1, 128), 1)
    experts = nz * npl
    total = jnp.where(lane < experts, total, -1.0)
    most = jnp.max(total, axis=1, keepdims=True)
    hot = jnp.min(jnp.where(total == most, lane.astype(F32), 1e6), axis=1, keepdims=True)

    n2 = npl * s2
    same_z = (iota((n2, cols), 0) % nz) == (iota((n2, cols), 1) // tok)
    holder = resident(n2, s2)
    copy_number = (iota((n2, cols), 0) // s1 % (COPIES + 1)).astype(F32)
    match = jnp.zeros((n2, cols), F32)
    gate = jnp.zeros((n2, cols), F32)
    for k in range(TOPK):
        chosen, pick = field(E2, k), field(PICK, k)
        number = jnp.where(chosen == hot, pick, 0.0)
        wanted = jnp.where(copy_number > 0.0, hot, holder)
        hit = (chosen == wanted) & (number == copy_number) & same_z
        match += hit.astype(F32)
        gate += jnp.where(hit, field(G2, k), 0.0)
    sel2 = selection(match, n2)
    here = jnp.where((copy_number == 0.0) | (holder == hot), sel2 * gate, 0.0)
    mixer2 = here.T
    sel2 = sel2.astype(BF16)

    for k in range(2, ring2.steps + 1):
        ring2.wait_recv(k - 1)
        ring2.start(k)

    x1.wait_recv()
    y1_y = go(Copies(ny, y, lambda o: mine(y1), lambda m: lanes(y1, m, feat), ydev, *pair()))

    ring2.wait_recv(ring2.steps)
    regular = jnp.concatenate([sel2[i * s2 : i * s2 + s1] for i in range(npl)], axis=0)
    extra = sel2[s1:s2]
    hot_rows = s2 - s1
    pieces = 2 * ny
    step = width // pieces
    for i in range(pieces):
        columns = slice(i * step, (i + 1) * step)
        xr2[pl.ds(p * s2 + s1, hot_rows), columns] = dot(extra, z2[:, columns]).astype(BF16)
    hot_block = lambda o: rows(xr2, o * s2 + s1, hot_rows)
    xc = lambda o: o * CORES + c
    ringh = Ring(
        nx,
        x,
        lambda i: hot_block(xc(i)),
        lambda i, h: block(xr2, xc(i) * s2 + s1, hot_rows, h * (width // 2), width // 2),
        xdev,
        *pair(),
    )
    ringh.start(1)
    for i in range(pieces):
        columns = slice(i * step, (i + 1) * step)
        xs2[:, columns] = dot(regular, z2[:, columns]).astype(BF16)
    x2 = go(Copies(npl, p, lambda o: rows(xs2, o * s1, s1), lambda m: rows(xr2, m * s2, s1), pdev, *pair()))
    xr2[pl.ds(p * s2, s1), :] = xs2[pl.ds(p * s1, s1), :]
    sib_send, sib_recv = pair()
    sibling = []

    def to_sibling(i):
        item = pltpu.make_async_remote_copy(
            src_ref=hot_block(xc(i)),
            dst_ref=hot_block(xc(i)),
            send_sem=sib_send.at[len(sibling)],
            recv_sem=sib_recv.at[len(sibling)],
            device_id=pdev(x * CORES + 1 - c),
            device_id_type=MESH,
        )
        item.start()
        sibling.append(item)

    to_sibling(x)

    def front(lhs, length):
        acc[pl.ds(0, length), :] = jnp.zeros((length, 2 * ff), F32)

        @pl.loop(0, ny)
        def _(q):
            part = pl.ds(pl.multiple_of(q * feat, feat), feat)
            a = lhs[:, part]
            for i in range(2):
                acc[pl.ds(0, length), i * ff : (i + 1) * ff] += dot(a, wgu[i, part, :])

    def active(hid, length):
        gated = acc[pl.ds(0, length), 0:ff]
        value = gated / (1.0 + jnp.exp(-gated)) * acc[pl.ds(0, length), ff : 2 * ff]
        hid[:, pl.ds(pl.multiple_of(y * ff, ff), ff)] = value.astype(BF16)

    def gather_hidden(hid):
        return go(Copies(ny, y, lambda o: lanes(hid, y, ff), lambda m: lanes(hid, m, ff), ydev, *pair()))

    weights.wait()
    y1_y.wait_recv()
    front(y1, n1)
    active(hid1, n1)
    hid1_y = gather_hidden(hid1)

    for k in range(1, ringh.steps + 1):
        ringh.wait_recv(k)
        if k < ringh.steps:
            ringh.start(k + 1)
            to_sibling(lax.rem(x + nx - k, nx))
            to_sibling(lax.rem(x + k, nx))
        else:
            to_sibling(lax.rem(x + k, nx))

    own_out.wait()
    out_y.wait_recv()
    hid1_y.wait_recv()
    o1[...] = dot(hid1[...], wd[...]).astype(BF16)
    r1 = go(
        Copies(npl, p, lambda o: rows(o1, o * s1, s1), lambda m: rows(ro1, m * s1, s1), pdev, *pair())
    )
    ro1[pl.ds(p * s1, s1), :] = o1[pl.ds(p * s1, s1), :]

    x2.wait_recv()
    for item in sibling:
        item.wait_recv()
    front(xr2, n2)
    active(hid2, n2)
    hid2_y = gather_hidden(hid2)

    def mix(mixer, ro, out, inbox):
        high = mixer.astype(BF16)
        low = (mixer - high.astype(F32)).astype(BF16)
        out[...] = (dot(high, ro[...]) + dot(low, ro[...])).astype(BF16)
        copies = go(
            Copies(nz, z, lambda o: rows(out, o * tok, tok), lambda m: rows(inbox, m * tok, tok), zdev, *pair())
        )
        inbox[pl.ds(z * tok, tok), :] = out[pl.ds(z * tok, tok), :]
        return copies

    r1.wait_recv()
    m1 = mix(mixer1, ro1, mix1, mr1)

    hid2_y.wait_recv()

    tile = min(n2, 128)

    @pl.loop(0, n2 // tile)
    def _(i):
        part = pl.ds(pl.multiple_of(i * tile, tile), tile)
        o2[part, :] = dot(hid2[part, :], wd[...]).astype(BF16)

    r2 = go(
        Copies(npl, p, lambda o: rows(o2, o * s2, s2), lambda m: rows(ro2, m * s2, s2), pdev, *pair())
    )
    ro2[pl.ds(p * s2, s2), :] = o2[pl.ds(p * s2, s2), :]

    def final(inbox, out):
        total = inbox[0:tok, :].astype(F32)
        for i in range(1, nz):
            total += inbox[i * tok : (i + 1) * tok, :].astype(F32)
        out[...] = total.astype(BF16)

    m1.wait_recv()
    final(mr1, out1)
    r2.wait_recv()
    m2 = mix(mixer2, ro2, mix2, mr2)
    m2.wait_recv()
    final(mr2, out2)

    for copies in started:
        copies.wait_send()
    ring2.wait_send()
    ringh.wait_send()
    for item in sibling:
        item.wait_send()


def shards(
    dims, tokens_one, experts_one, gates_one, tokens_two, experts_two, gates_two, replica_pick, home, w_gate_up, w_down
):
    nz, nx, ny = dims
    npl = nx * CORES
    tok, feat = tokens_one.shape
    width = feat * ny
    ff = w_gate_up.shape[3]
    info = jnp.concatenate(
        [
            experts_one.astype(F32),
            gates_one,
            experts_two.astype(F32),
            gates_two,
            (replica_pick % (COPIES + 1)).astype(F32),
            jnp.zeros((tok, 128 - 5 * TOPK), F32),
        ],
        axis=1,
    )
    home = jnp.pad(home[None, :], ((0, 7), (0, 128 - home.shape[0])), constant_values=-1)
    cols = nz * tok
    n1 = npl * SLOT * nz
    n2 = n1 * (COPIES + 1)
    vmem = pltpu.VMEM
    dma = pltpu.SemaphoreType.DMA
    groups = [nz, ny, nz, nz + 2, ny, npl, npl, ny, nx + 2, npl, nx, ny, npl, ny, nz, npl, nz]
    any_spec = pl.BlockSpec(memory_space=pl.ANY)
    in_vmem = pl.BlockSpec(memory_space=pltpu.VMEM)
    return pl.pallas_call(
        functools.partial(kernel, dims),
        out_shape=[jax.ShapeDtypeStruct((tok, feat), BF16)] * 2,
        in_specs=[in_vmem] * 4 + [any_spec] * 2,
        out_specs=[in_vmem] * 2,
        scratch_shapes=[
            vmem((cols, feat), BF16),
            vmem((cols, width), BF16),
            vmem((cols, 128), F32),
            vmem((npl * 8, 128), F32),
            vmem((n1, feat), BF16),
            vmem((n1, width), BF16),
            vmem((n1, width), BF16),
            vmem((n2, width), BF16),
            vmem((n1, ff * ny), BF16),
            vmem((n2, ff * ny), BF16),
            vmem(w_gate_up.shape[1:], BF16),
            vmem((ff * ny, feat), BF16),
            vmem((n2, 2 * ff), F32),
            vmem((n1, feat), BF16),
            vmem((n2, feat), BF16),
            vmem((n1, feat), BF16),
            vmem((n2, feat), BF16),
            vmem((cols, feat), BF16),
            vmem((cols, feat), BF16),
            vmem((cols, feat), BF16),
            vmem((cols, feat), BF16),
            dma((2,)),
        ]
        + [dma((n + 2,)) for n in groups for _ in range(2)],
        compiler_params=pltpu.CompilerParams(
            collective_id=0, has_side_effects=True, vmem_limit_bytes=56 * 1024 * 1024
        ),
        cost_estimate=pl.CostEstimate(flops=10_000_000_000, bytes_accessed=16_000_000, transcendentals=0),
    )(tokens_one, tokens_two, info, home, w_gate_up, w_down)


def solution(mesh):
    placed = (
        P("expert", "inner"),
        P("expert", None),
        P("expert", None),
        P("expert", "inner"),
        P("expert", None),
        P("expert", None),
        P("expert", None),
        P(),
        P("expert", None, None, "inner"),
        P("expert", "inner", None),
    )
    experts, inner = mesh.shape["expert"], mesh.shape["inner"]
    nx = 4 if experts >= 16 else 2
    dims = (experts // (nx * CORES), nx, inner)
    return jax.shard_map(
        functools.partial(shards, dims),
        mesh=mesh,
        in_specs=placed,
        out_specs=(P("expert", "inner"), P("expert", "inner")),
        check_vma=False,
    )
```

```python
import functools

import jax
import jax.numpy as jnp
from jax import lax
from jax.experimental import pallas as pl
from jax.experimental.pallas import tpu as pltpu
from jax.sharding import PartitionSpec as P

MESH = pl.DeviceIdType.MESH
TOPK = 8
COPIES = 3
SLOT = 2
CORES = 2
F32 = jnp.float32
BF16 = jnp.bfloat16
E1, G1, E2, G2, PICK = 0, 8, 16, 24, 32


def dot(a, b):
    return jnp.dot(a, b, preferred_element_type=F32)


def iota(shape, dim):
    return lax.broadcasted_iota(jnp.int32, shape, dim)


class Copies:
    def __init__(self, n, me, src, dst, device, send, recv):
        self.items = []
        for i in range(1, n):
            peer = lax.rem(me + i, n)
            self.items.append(
                pltpu.make_async_remote_copy(
                    src_ref=src(peer),
                    dst_ref=dst(me),
                    send_sem=send.at[i],
                    recv_sem=recv.at[i],
                    device_id=device(peer),
                    device_id_type=MESH,
                )
            )

    def start(self):
        for item in self.items:
            item.start()

    def wait_from(self, ahead):
        self.items[len(self.items) - ahead].wait_recv()

    def wait_recv(self):
        for item in self.items:
            item.wait_recv()

    def wait_send(self):
        for item in self.items:
            item.wait_send()


class Ring:
    def __init__(self, n, me, block, half, device, send, recv):
        self.steps = n // 2
        self.at = 0
        self.pairs = []
        right, left = lax.rem(me + 1, n), lax.rem(me + n - 1, n)
        for k in range(1, self.steps + 1):
            pair = []
            for way, (target, index) in enumerate(
                ((right, lax.rem(me + n - (k - 1), n)), (left, lax.rem(me + (k - 1), n)))
            ):
                ref = half(index, way) if k == self.steps else block(index)
                pair.append(
                    pltpu.make_async_remote_copy(
                        src_ref=ref,
                        dst_ref=ref,
                        send_sem=send.at[2 * k + way],
                        recv_sem=recv.at[2 * k + way],
                        device_id=device(target),
                        device_id_type=MESH,
                    )
                )
            self.pairs.append(pair)

    def step(self):
        if self.at > self.steps:
            return
        if self.at > 0:
            for item in self.pairs[self.at - 1]:
                item.wait_recv()
        if self.at < self.steps:
            for item in self.pairs[self.at]:
                item.start()
        self.at += 1

    def finish(self):
        while self.at <= self.steps:
            self.step()

    def wait_send(self):
        for pair in self.pairs:
            for item in pair:
                item.wait_send()


def kernel(
    dims,
    tok1,
    tok2,
    e1,
    g1,
    e2,
    g2,
    picks,
    home,
    w_in,
    w_out,
    out,
    pack,
    info,
    counts,
    z1,
    z2,
    xs1,
    xs2,
    xr,
    acc,
    hid,
    o,
    ro,
    blend,
    mix,
    inbox,
    halves,
    wgu,
    wd,
    local,
    *sems,
):
    nz, nx, ny = dims
    npl = nx * CORES
    tok, feat = tok1.shape
    width = feat * ny
    ff = w_in.shape[3]
    cols = nz * tok
    s1 = SLOT * nz
    chunk = npl * s1
    sems = list(sems)

    e = lax.axis_index("expert")
    y = lax.axis_index("inner")
    z = e // npl
    p = lax.rem(e, npl)
    x = p // CORES
    c = lax.rem(p, CORES)
    zdev = lambda other: (other * npl + p, y)
    pdev = lambda other: (z * npl + other, y)
    ydev = lambda other: (e, other)
    xdev = lambda other: (z * npl + other * CORES + c, y)

    def pair():
        return sems.pop(0), sems.pop(0)

    def rows(ref, start, size):
        return ref.at[pl.ds(start, size)]

    def lanes(ref, index, size):
        return ref.at[:, pl.ds(pl.multiple_of(index * size, size), size)]

    def block(ref, r, rs, l, ls):
        return ref.at[pl.ds(r, rs), pl.ds(pl.multiple_of(l, ls), ls)]

    weights = pltpu.make_async_copy(w_in.at[0], wgu, local.at[0])
    weights.start()
    own_out = pltpu.make_async_copy(lanes(w_out.at[0], y, feat), rows(wd, y * ff, ff), local.at[1])
    own_out.start()

    pack[...] = jnp.zeros_like(pack)
    pack[E1 : E1 + TOPK, 0:tok] = e1[...].astype(F32)
    pack[G1 : G1 + TOPK, 0:tok] = g1[...]
    pack[E2 : E2 + TOPK, 0:tok] = e2[...].astype(F32)
    pack[G2 : G2 + TOPK, 0:tok] = g2[...]
    pack[PICK : PICK + TOPK, 0:tok] = lax.rem(picks[...], COPIES + 1).astype(F32)
    info[pl.ds(z * tok, tok), :] = pack[...].T[0:tok, :]
    z1[pl.ds(z * tok, tok), :] = tok1[...]
    z2[pl.ds(z * tok, tok), pl.ds(pl.multiple_of(y * feat, feat), feat)] = tok2[...]

    barrier = pltpu.get_barrier_semaphore()
    for i in range(1, nz):
        pl.semaphore_signal(barrier, inc=1, device_id=zdev(lax.rem(z + i, nz)), device_id_type=MESH)
    for i in range(1, npl):
        pl.semaphore_signal(barrier, inc=1, device_id=pdev(lax.rem(p + i, npl)), device_id_type=MESH)
    for i in range(1, ny):
        pl.semaphore_signal(barrier, inc=1, device_id=ydev(lax.rem(y + i, ny)), device_id_type=MESH)

    shape = (cols, cols)
    earlier = ((iota(shape, 0) // tok == iota(shape, 1) // tok) & (iota(shape, 0) < iota(shape, 1))).astype(BF16)
    here = home.shape[1]
    held = home[0:1, :] == z * npl + iota((chunk, here), 0) // s1
    holder = jnp.sum(jnp.where(held, iota((chunk, here), 1).astype(F32), 0.0), axis=1, keepdims=True)

    pl.semaphore_wait(barrier, nz + npl + ny - 3)

    started = []

    def go(copies):
        copies.start()
        started.append(copies)
        return copies

    order = [0, 1, 3, 2] if ny == 4 else list(range(ny))
    quarters = [lax.rem(y + s, ny) for s in order]
    rings = [
        Ring(
            nz,
            z,
            lambda i, q=q: block(z2, i * tok, tok, q * feat, feat),
            lambda i, h, q=q: block(z2, i * tok, tok, q * feat + h * (feat // 2), feat // 2),
            zdev,
            *pair(),
        )
        for q in quarters
    ]
    rings.append(
        Ring(
            nz,
            z,
            lambda i: rows(z1, i * tok, tok),
            lambda i, h: block(z1, i * tok, tok, h * (feat // 2), feat // 2),
            zdev,
            *pair(),
        )
    )
    rings[0].step()
    rings[ny].step()
    info_z = go(
        Copies(nz, z, lambda i: rows(info, z * tok, tok), lambda m: rows(info, m * tok, tok), zdev, *pair())
    )
    tok2_y = go(Copies(ny, y, lambda i: tok2, lambda m: lanes(rows(z2, z * tok, tok), m, feat), ydev, *pair()))
    out_y = go(
        Copies(ny, y, lambda i: lanes(w_out.at[0], i, feat), lambda m: rows(wd, m * ff, ff), ydev, *pair())
    )

    def tick(some):
        for ring in some:
            ring.step()

    info_z.wait_recv()
    every = info[...]
    turned = every.T
    field = lambda base, k: turned[base + k : base + k + 1, :]
    expert_lane = iota((cols, 128), 1).astype(F32)
    tally = jnp.zeros((cols, 128), F32)
    for k in range(TOPK):
        tally += (every[:, E1 + k : E1 + k + 1] == expert_lane).astype(F32)
    counts[pl.ds(p * 8, 8), :] = jnp.broadcast_to(jnp.sum(tally, axis=0, keepdims=True), (8, 128))
    counts_p = go(
        Copies(npl, p, lambda i: rows(counts, p * 8, 8), lambda m: rows(counts, m * 8, 8), pdev, *pair())
    )
    tick([rings[0], rings[ny]])
    tok2_y.wait_recv()
    tick(rings[1:ny])

    def selection(match, length):
        number = dot(match.astype(BF16), earlier)
        slot = (iota((length, cols), 0) // nz % SLOT).astype(F32)
        return jnp.where(number == slot, match, 0.0)

    def sourced(length):
        return (iota((length, cols), 0) % nz) == (iota((length, cols), 1) // tok)

    same_z = sourced(chunk)
    match = jnp.zeros((chunk, cols), F32)
    gate = jnp.zeros((chunk, cols), F32)
    for k in range(TOPK):
        hit = (field(E1, k) == holder) & same_z
        match += hit.astype(F32)
        gate += jnp.where(hit, field(G1, k), 0.0)
    sel1 = selection(match, chunk)
    mixers = [(sel1 * gate).T]
    sel1 = sel1.astype(BF16)
    tick(rings)
    counts_p.wait_recv()
    total = counts[0:8, :]
    for other in range(1, npl):
        total += counts[other * 8 : other * 8 + 8, :]
    lane = iota((1, 128), 1)
    total = jnp.where(lane < nz * npl, total[0:1, :], -1.0)
    most = jnp.max(total, axis=1, keepdims=True)
    hot = jnp.min(jnp.where(total == most, lane.astype(F32), 1e6), axis=1, keepdims=True)

    match = jnp.zeros((chunk, cols), F32)
    gate = jnp.zeros((chunk, cols), F32)
    for k in range(TOPK):
        chosen, pick = field(E2, k), field(PICK, k)
        hit = (chosen == holder) & ((chosen != hot) | (pick == 0.0)) & same_z
        match += hit.astype(F32)
        gate += jnp.where(hit, field(G2, k), 0.0)
    sel2 = selection(match, chunk)
    mixer2 = (sel2 * gate).T
    sel2 = sel2.astype(BF16)
    tick(rings)

    rings[ny].finish()
    xs1[...] = dot(sel1, z1[...]).astype(BF16)
    mine = lambda ref: lanes(ref, y, feat)
    x1 = go(
        Copies(npl, p, lambda i: rows(xs1, i * s1, s1), lambda m: mine(rows(xr, m * s1, s1)), pdev, *pair())
    )
    xr[pl.ds(p * s1, s1), pl.ds(pl.multiple_of(y * feat, feat), feat)] = xs1[pl.ds(p * s1, s1), :]
    tick(rings[1:ny])

    hots = COPIES * s1
    copy_number = (iota((hots, cols), 0) // s1 + 1).astype(F32)
    same_copy = sourced(hots)
    match = jnp.zeros((hots, cols), F32)
    gate = jnp.zeros((hots, cols), F32)
    for k in range(TOPK):
        hit = (field(E2, k) == hot) & (field(PICK, k) == copy_number) & same_copy
        match += hit.astype(F32)
        gate += jnp.where(hit, field(G2, k), 0.0)
    selh = selection(match, hots)
    gated = selh * gate
    chip = z * nx + iota((chunk, here), 0) // s1
    on_chip = (home[0:1, :] // CORES == chip) & (iota((chunk, here), 0) < nx * s1)
    total = jnp.where(on_chip & (iota((chunk, here), 1).astype(F32) == hot), 1.0, 0.0)
    chip_hot = jnp.sum(total, axis=1, keepdims=True) > 0.0
    own = jnp.where((home[0:1, :] == e) & (iota((1, here), 1).astype(F32) == hot), 1.0, 0.0)
    own_hot = jnp.sum(own, axis=1, keepdims=True) > 0.0
    mixers.append(mixer2)
    for j in range(COPIES):
        tiled = jnp.concatenate([gated[j * s1 : (j + 1) * s1]] * npl, axis=0)
        mixers.append(jnp.where(chip_hot, tiled, 0.0).T)
    selh = selh.astype(BF16)

    def exchange(s):
        q = quarters[s]
        part = pl.ds(pl.multiple_of(q * feat, feat), feat)
        xs2[:, part] = dot(sel2, z2[:, part]).astype(BF16)
        copies = go(
            Copies(
                npl,
                p,
                lambda i: block(xs2, i * s1, s1, q * feat, feat),
                lambda m: block(xr, chunk + m * s1, s1, q * feat, feat),
                pdev,
                *pair(),
            )
        )
        xr[pl.ds(chunk + p * s1, s1), part] = xs2[pl.ds(p * s1, s1), part]
        return copies

    x2 = []
    for s in range(ny):
        rings[s].finish()
        x2.append(exchange(s))
        tick(rings[s + 1 : ny])

    hot_base = lambda j, i, core: (2 + j) * chunk + (core * nx + i) * s1
    hot_rings, siblings = [], []
    for j in range(COPIES):
        for s in range(ny):
            part = slice(s * feat, (s + 1) * feat)
            xr[pl.ds(hot_base(j, x, c), s1), part] = dot(selh[j * s1 : (j + 1) * s1], z2[:, part]).astype(BF16)
        hot_rings.append(
            Ring(
                nx,
                x,
                lambda i, j=j: rows(xr, hot_base(j, i, c), s1),
                lambda i, h, j=j: block(xr, hot_base(j, i, c), s1, h * (width // 2), width // 2),
                xdev,
                *pair(),
            )
        )
        siblings.append(([], *pair()))

    def to_sibling(j, i):
        items, send, recv = siblings[j]
        ref = rows(xr, hot_base(j, i, c), s1)
        item = pltpu.make_async_remote_copy(
            src_ref=ref,
            dst_ref=ref,
            send_sem=send.at[len(items)],
            recv_sem=recv.at[len(items)],
            device_id=pdev(x * CORES + 1 - c),
            device_id_type=MESH,
        )
        item.start()
        items.append(item)

    def hot_step(j):
        ring = hot_rings[j]
        k = ring.at
        ring.step()
        if k == 0:
            to_sibling(j, x)
        elif k < ring.steps:
            to_sibling(j, lax.rem(x + nx - k, nx))
            to_sibling(j, lax.rem(x + k, nx))
        else:
            to_sibling(j, lax.rem(x + k, nx))

    def hot_arrived(j):
        while hot_rings[j].at <= hot_rings[j].steps:
            hot_step(j)
        for item in siblings[j][0]:
            item.wait_recv()

    def front(i):
        part = pl.ds(i * chunk, chunk)
        acc[...] = jnp.zeros_like(acc)

        @pl.loop(0, ny)
        def _(q):
            features = pl.ds(pl.multiple_of(q * feat, feat), feat)
            a = xr[part, features]
            for half in range(2):
                acc[:, half * ff : (half + 1) * ff] += dot(a, wgu[half, features, :])

        gated = acc[:, 0:ff]
        value = gated / (1.0 + jnp.exp(-gated)) * acc[:, ff : 2 * ff]
        hid[part, pl.ds(pl.multiple_of(y * ff, ff), ff)] = value.astype(BF16)
        ref = block(hid, i * chunk, chunk, y * ff, ff)
        return go(Copies(ny, y, lambda m: ref, lambda m: block(hid, i * chunk, chunk, m * ff, ff), ydev, *pair()))

    def back(i, gathered):
        gathered.wait_recv()
        part = pl.ds(i * chunk, chunk)
        o[part, :] = dot(hid[part, :], wd[...]).astype(BF16)
        own = pl.ds(i * chunk + p * s1, s1)
        ro[own, :] = o[own, :]
        return go(
            Copies(
                npl,
                p,
                lambda m: rows(o, i * chunk + m * s1, s1),
                lambda m: rows(ro, i * chunk + m * s1, s1),
                pdev,
                *pair(),
            )
        )

    def back_hot(i, gathered):
        gathered.wait_recv()
        part = pl.ds(i * chunk, chunk)
        o[part, :] = jnp.where(own_hot, dot(hid[part, :], wd[...]), 0.0).astype(BF16)
        half = nx * s1
        away = rows(o, i * chunk + (1 - c) * half, half)
        item = pltpu.make_async_remote_copy(
            src_ref=away,
            dst_ref=rows(halves, (i - 2) * half, half),
            send_sem=half_send.at[i - 2],
            recv_sem=half_recv.at[i - 2],
            device_id=pdev(x * CORES + 1 - c),
            device_id_type=MESH,
        )
        item.start()
        siblings.append(([item], None, None))
        return item

    def back_chip(i, item):
        item.wait_recv()
        half = nx * s1
        kept = pl.ds(i * chunk + c * half, half)
        o[kept, :] += halves[pl.ds((i - 2) * half, half), :]
        own = pl.ds(i * chunk + x * s1, s1)
        ro[own, :] = o[pl.ds(i * chunk + c * half + x * s1, s1), :]
        return go(
            Copies(
                nx,
                x,
                lambda m: rows(o, i * chunk + c * half + m * s1, s1),
                lambda m: rows(ro, i * chunk + m * s1, s1),
                xdev,
                *pair(),
            )
        )

    def mixed(i, returned):
        returned.wait_recv()
        high = mixers[i].astype(BF16)
        low = (mixers[i] - high.astype(F32)).astype(BF16)
        used = nx * s1 if i > 1 else chunk
        both = jnp.concatenate([high[:, 0:used], low[:, 0:used]], axis=0)
        sums = dot(both, ro[pl.ds(i * chunk, used), :])
        return sums[0:cols] + sums[cols:]

    def deliver(b):
        copies = go(
            Copies(
                nz,
                z,
                lambda m: rows(mix, b * cols + m * tok, tok),
                lambda m: rows(inbox, b * cols + m * tok, tok),
                zdev,
                *pair(),
            )
        )
        own = pl.ds(b * cols + z * tok, tok)
        inbox[own, :] = mix[own, :]
        return copies

    def final(b, copies):
        copies.wait_recv()
        total = inbox[b * cols : b * cols + tok, :].astype(F32)
        for i in range(1, nz):
            start = b * cols + i * tok
            total += inbox[start : start + tok, :].astype(F32)
        out[b * tok : (b + 1) * tok, :] = total

    half_send, half_recv = pair()
    hot_step(0)
    hot_step(1)
    x1.wait_recv()
    y1 = go(Copies(ny, y, lambda i: mine(rows(xr, 0, chunk)), lambda m: lanes(rows(xr, 0, chunk), m, feat), ydev, *pair()))

    weights.wait()
    for copies in x2:
        copies.wait_recv()
    h1 = front(1)
    hot_step(0)
    hot_step(2)
    hot_step(1)
    hot_arrived(0)
    h2 = front(2)
    hot_step(2)
    own_out.wait()
    out_y.wait_recv()
    r1 = back(1, h1)
    hot_arrived(1)
    h3 = front(3)
    b2 = back_hot(2, h2)
    hot_arrived(2)
    h4 = front(4)
    r2 = back_chip(2, b2)
    b3 = back_hot(3, h3)
    y1.wait_recv()
    h0 = front(0)
    r3 = back_chip(3, b3)
    b4 = back_hot(4, h4)
    blend[...] = mixed(1, r1)
    r4 = back_chip(4, b4)
    r0 = back(0, h0)
    blend[...] += mixed(2, r2)
    blend[...] += mixed(3, r3)
    mix[cols : 2 * cols, :] = (blend[...] + mixed(4, r4)).astype(BF16)
    d2 = deliver(1)
    mix[0:cols, :] = mixed(0, r0).astype(BF16)
    d1 = deliver(0)
    final(1, d2)
    final(0, d1)

    for copies in started + rings + hot_rings:
        copies.wait_send()
    for items, _, _ in siblings:
        for item in items:
            item.wait_send()


def shards(
    dims, tokens_one, experts_one, gates_one, tokens_two, experts_two, gates_two, replica_pick, home, w_gate_up, w_down
):
    nz, nx, ny = dims
    npl = nx * CORES
    tok, feat = tokens_one.shape
    width = feat * ny
    ff = w_gate_up.shape[3]
    cols = nz * tok
    chunk = npl * SLOT * nz
    chunks = 2 + COPIES
    vmem = pltpu.VMEM
    dma = pltpu.SemaphoreType.DMA
    size = max(nz, npl, ny, nx) + 4
    groups = 1 + 2 + ny + 2 + 1 + 1 + 2 + ny + 2 * COPIES + 1 + 1 + 2 * chunks + 2
    any_spec = pl.BlockSpec(memory_space=pl.ANY)
    in_vmem = pl.BlockSpec(memory_space=pltpu.VMEM)
    out = pl.pallas_call(
        functools.partial(kernel, dims),
        out_shape=jax.ShapeDtypeStruct((2 * tok, feat), F32),
        in_specs=[in_vmem] * 8 + [any_spec] * 2,
        out_specs=in_vmem,
        scratch_shapes=[
            vmem((128, 128), F32),
            vmem((cols, 128), F32),
            vmem((npl * 8, 128), F32),
            vmem((cols, feat), BF16),
            vmem((cols, width), BF16),
            vmem((chunk, feat), BF16),
            vmem((chunk, width), BF16),
            vmem((chunks * chunk, width), BF16),
            vmem((chunk, 2 * ff), F32),
            vmem((chunks * chunk, ff * ny), BF16),
            vmem((chunks * chunk, feat), BF16),
            vmem((chunks * chunk, feat), BF16),
            vmem((cols, feat), F32),
            vmem((2 * cols, feat), BF16),
            vmem((2 * cols, feat), BF16),
            vmem((COPIES * nx * SLOT * nz, feat), BF16),
            vmem(w_gate_up.shape[1:], BF16),
            vmem((ff * ny, feat), BF16),
            dma((2,)),
        ]
        + [dma((size,)) for _ in range(2 * groups)],
        compiler_params=pltpu.CompilerParams(
            collective_id=0, has_side_effects=True, vmem_limit_bytes=56 * 1024 * 1024
        ),
        cost_estimate=pl.CostEstimate(flops=10_000_000_000, bytes_accessed=16_000_000, transcendentals=0),
    )(
        tokens_one,
        tokens_two,
        experts_one.T,
        gates_one.T,
        experts_two.T,
        gates_two.T,
        replica_pick.T,
        home[None, :],
        w_gate_up,
        w_down,
    )
    return out[:tok].astype(BF16), out[tok:].astype(BF16)


def solution(mesh):
    placed = (
        P("expert", "inner"),
        P("expert", None),
        P("expert", None),
        P("expert", "inner"),
        P("expert", None),
        P("expert", None),
        P("expert", None),
        P(),
        P("expert", None, None, "inner"),
        P("expert", "inner", None),
    )
    experts, inner = mesh.shape["expert"], mesh.shape["inner"]
    nx = 4 if experts >= 16 else 2
    dims = (experts // (nx * CORES), nx, inner)
    return jax.shard_map(
        functools.partial(shards, dims),
        mesh=mesh,
        in_specs=placed,
        out_specs=(P("expert", "inner"), P("expert", "inner")),
        check_vma=False,
    )
```

```python
import functools

import jax
import jax.numpy as jnp
from jax import lax
from jax.experimental import pallas as pl
from jax.experimental.pallas import tpu as pltpu
from jax.sharding import PartitionSpec as P

MESH = pl.DeviceIdType.MESH
TOPK = 8
COPIES = 3
SLOT = 2
CORES = 2
F32 = jnp.float32
BF16 = jnp.bfloat16
E1, G1, E2, G2, PICK = 0, 8, 16, 24, 32


def dot(a, b):
    return jnp.dot(a, b, preferred_element_type=F32)


def iota(shape, dim):
    return lax.broadcasted_iota(jnp.int32, shape, dim)


class Copies:
    def __init__(self, n, me, src, dst, device, send, recv):
        self.items = []
        for i in range(1, n):
            peer = lax.rem(me + i, n)
            self.items.append(
                pltpu.make_async_remote_copy(
                    src_ref=src(peer),
                    dst_ref=dst(me),
                    send_sem=send.at[i],
                    recv_sem=recv.at[i],
                    device_id=device(peer),
                    device_id_type=MESH,
                )
            )

    def start(self):
        for item in self.items:
            item.start()

    def wait_from(self, ahead):
        self.items[len(self.items) - ahead].wait_recv()

    def wait_recv(self):
        for item in self.items:
            item.wait_recv()

    def wait_send(self):
        for item in self.items:
            item.wait_send()


class Ring:
    def __init__(self, n, me, block, half, device, send, recv):
        self.steps = n // 2
        self.at = 0
        self.pairs = []
        right, left = lax.rem(me + 1, n), lax.rem(me + n - 1, n)
        for k in range(1, self.steps + 1):
            pair = []
            for way, (target, index) in enumerate(
                ((right, lax.rem(me + n - (k - 1), n)), (left, lax.rem(me + (k - 1), n)))
            ):
                ref = half(index, way) if k == self.steps else block(index)
                pair.append(
                    pltpu.make_async_remote_copy(
                        src_ref=ref,
                        dst_ref=ref,
                        send_sem=send.at[2 * k + way],
                        recv_sem=recv.at[2 * k + way],
                        device_id=device(target),
                        device_id_type=MESH,
                    )
                )
            self.pairs.append(pair)

    def step(self):
        if self.at > self.steps:
            return
        if self.at > 0:
            for item in self.pairs[self.at - 1]:
                item.wait_recv()
        if self.at < self.steps:
            for item in self.pairs[self.at]:
                item.start()
        self.at += 1

    def finish(self):
        while self.at <= self.steps:
            self.step()

    def wait_send(self):
        for pair in self.pairs:
            for item in pair:
                item.wait_send()


def kernel(
    dims,
    tok1,
    tok2,
    e1,
    g1,
    e2,
    g2,
    picks,
    home,
    w_in,
    w_out,
    out,
    pack,
    info,
    counts,
    z1,
    z2,
    xs1,
    xs2,
    xr,
    acc,
    hid,
    o,
    ro,
    blend,
    mix,
    inbox,
    halves,
    wgu,
    wd,
    local,
    *sems,
):
    nz, nx, ny = dims
    npl = nx * CORES
    tok, feat = tok1.shape
    width = feat * ny
    ff = w_in.shape[3]
    cols = nz * tok
    s1 = SLOT * nz
    chunk = npl * s1
    sems = list(sems)

    e = lax.axis_index("expert")
    y = lax.axis_index("inner")
    z = e // npl
    p = lax.rem(e, npl)
    x = p // CORES
    c = lax.rem(p, CORES)
    zdev = lambda other: (other * npl + p, y)
    pdev = lambda other: (z * npl + other, y)
    ydev = lambda other: (e, other)
    xdev = lambda other: (z * npl + other * CORES + c, y)

    def pair():
        return sems.pop(0), sems.pop(0)

    def rows(ref, start, size):
        return ref.at[pl.ds(start, size)]

    def lanes(ref, index, size):
        return ref.at[:, pl.ds(pl.multiple_of(index * size, size), size)]

    def block(ref, r, rs, l, ls):
        return ref.at[pl.ds(r, rs), pl.ds(pl.multiple_of(l, ls), ls)]

    weights = pltpu.make_async_copy(w_in.at[0], wgu, local.at[0])
    weights.start()
    own_out = pltpu.make_async_copy(lanes(w_out.at[0], y, feat), rows(wd, y * ff, ff), local.at[1])
    own_out.start()

    pack[...] = jnp.zeros_like(pack)
    pack[E1 : E1 + TOPK, 0:tok] = e1[...].astype(F32)
    pack[G1 : G1 + TOPK, 0:tok] = g1[...]
    pack[E2 : E2 + TOPK, 0:tok] = e2[...].astype(F32)
    pack[G2 : G2 + TOPK, 0:tok] = g2[...]
    pack[PICK : PICK + TOPK, 0:tok] = lax.rem(picks[...], COPIES + 1).astype(F32)
    info[pl.ds(z * tok, tok), :] = pack[...].T[0:tok, :]
    z1[pl.ds(z * tok, tok), :] = tok1[...]
    z2[pl.ds(z * tok, tok), pl.ds(pl.multiple_of(y * feat, feat), feat)] = tok2[...]

    barrier = pltpu.get_barrier_semaphore()
    for i in range(1, nz):
        pl.semaphore_signal(barrier, inc=1, device_id=zdev(lax.rem(z + i, nz)), device_id_type=MESH)
    for i in range(1, npl):
        pl.semaphore_signal(barrier, inc=1, device_id=pdev(lax.rem(p + i, npl)), device_id_type=MESH)
    for i in range(1, ny):
        pl.semaphore_signal(barrier, inc=1, device_id=ydev(lax.rem(y + i, ny)), device_id_type=MESH)

    shape = (cols, cols)
    earlier = ((iota(shape, 0) // tok == iota(shape, 1) // tok) & (iota(shape, 0) < iota(shape, 1))).astype(BF16)
    here = home.shape[1]
    held = home[0:1, :] == z * npl + iota((chunk, here), 0) // s1
    holder = jnp.sum(jnp.where(held, iota((chunk, here), 1).astype(F32), 0.0), axis=1, keepdims=True)

    pl.semaphore_wait(barrier, nz + npl + ny - 3)

    started = []

    def go(copies):
        copies.start()
        started.append(copies)
        return copies

    order = [0, 1, 3, 2] if ny == 4 else list(range(ny))
    quarters = [lax.rem(y + s, ny) for s in order]
    rings = [
        Ring(
            nz,
            z,
            lambda i, q=q: block(z2, i * tok, tok, q * feat, feat),
            lambda i, h, q=q: block(z2, i * tok, tok, q * feat + h * (feat // 2), feat // 2),
            zdev,
            *pair(),
        )
        for q in quarters
    ]
    rings.append(
        Ring(
            nz,
            z,
            lambda i: rows(z1, i * tok, tok),
            lambda i, h: block(z1, i * tok, tok, h * (feat // 2), feat // 2),
            zdev,
            *pair(),
        )
    )
    tok2_y = go(Copies(ny, y, lambda i: tok2, lambda m: lanes(rows(z2, z * tok, tok), m, feat), ydev, *pair()))
    rings[0].step()
    rings[ny].step()
    info_z = go(
        Copies(nz, z, lambda i: rows(info, z * tok, tok), lambda m: rows(info, m * tok, tok), zdev, *pair())
    )

    def tick(some):
        for ring in some:
            ring.step()

    tok2_y.wait_recv()
    tick(rings[1:ny])
    out_y = go(
        Copies(ny, y, lambda i: lanes(w_out.at[0], i, feat), lambda m: rows(wd, m * ff, ff), ydev, *pair())
    )

    info_z.wait_recv()
    every = info[...]
    turned = every.T
    field = lambda base, k: turned[base + k : base + k + 1, :]
    expert_lane = iota((cols, 128), 1).astype(F32)
    tally = jnp.zeros((cols, 128), F32)
    for k in range(TOPK):
        tally += (every[:, E1 + k : E1 + k + 1] == expert_lane).astype(F32)
    counts[pl.ds(p * 8, 8), :] = jnp.broadcast_to(jnp.sum(tally, axis=0, keepdims=True), (8, 128))
    counts_p = go(
        Copies(npl, p, lambda i: rows(counts, p * 8, 8), lambda m: rows(counts, m * 8, 8), pdev, *pair())
    )
    tick([rings[0], rings[ny]])

    def selection(match, length):
        number = dot(match.astype(BF16), earlier)
        slot = (iota((length, cols), 0) // nz % SLOT).astype(F32)
        return jnp.where(number == slot, match, 0.0)

    def sourced(length):
        return (iota((length, cols), 0) % nz) == (iota((length, cols), 1) // tok)

    same_z = sourced(chunk)
    match = jnp.zeros((chunk, cols), F32)
    gate = jnp.zeros((chunk, cols), F32)
    for k in range(TOPK):
        hit = (field(E1, k) == holder) & same_z
        match += hit.astype(F32)
        gate += jnp.where(hit, field(G1, k), 0.0)
    sel1 = selection(match, chunk)
    mixers = [(sel1 * gate).T]
    sel1 = sel1.astype(BF16)
    tick(rings)
    counts_p.wait_recv()
    total = counts[0:8, :]
    for other in range(1, npl):
        total += counts[other * 8 : other * 8 + 8, :]
    lane = iota((1, 128), 1)
    total = jnp.where(lane < nz * npl, total[0:1, :], -1.0)
    most = jnp.max(total, axis=1, keepdims=True)
    hot = jnp.min(jnp.where(total == most, lane.astype(F32), 1e6), axis=1, keepdims=True)

    match = jnp.zeros((chunk, cols), F32)
    gate = jnp.zeros((chunk, cols), F32)
    for k in range(TOPK):
        chosen, pick = field(E2, k), field(PICK, k)
        hit = (chosen == holder) & ((chosen != hot) | (pick == 0.0)) & same_z
        match += hit.astype(F32)
        gate += jnp.where(hit, field(G2, k), 0.0)
    sel2 = selection(match, chunk)
    mixer2 = (sel2 * gate).T
    sel2 = sel2.astype(BF16)
    tick(rings)

    rings[ny].finish()
    xs1[...] = dot(sel1, z1[...]).astype(BF16)
    mine = lambda ref: lanes(ref, y, feat)
    x1 = go(
        Copies(npl, p, lambda i: rows(xs1, i * s1, s1), lambda m: mine(rows(xr, m * s1, s1)), pdev, *pair())
    )
    xr[pl.ds(p * s1, s1), pl.ds(pl.multiple_of(y * feat, feat), feat)] = xs1[pl.ds(p * s1, s1), :]
    tick(rings[1:ny])

    hots = COPIES * s1
    copy_number = (iota((hots, cols), 0) // s1 + 1).astype(F32)
    same_copy = sourced(hots)
    match = jnp.zeros((hots, cols), F32)
    gate = jnp.zeros((hots, cols), F32)
    for k in range(TOPK):
        hit = (field(E2, k) == hot) & (field(PICK, k) == copy_number) & same_copy
        match += hit.astype(F32)
        gate += jnp.where(hit, field(G2, k), 0.0)
    selh = selection(match, hots)
    gated = selh * gate
    chip = z * nx + iota((chunk, here), 0) // s1
    on_chip = (home[0:1, :] // CORES == chip) & (iota((chunk, here), 0) < nx * s1)
    total = jnp.where(on_chip & (iota((chunk, here), 1).astype(F32) == hot), 1.0, 0.0)
    chip_hot = jnp.sum(total, axis=1, keepdims=True) > 0.0
    own = jnp.where((home[0:1, :] == e) & (iota((1, here), 1).astype(F32) == hot), 1.0, 0.0)
    own_hot = jnp.sum(own, axis=1, keepdims=True) > 0.0
    mixers.append(mixer2)
    for j in range(COPIES):
        tiled = jnp.concatenate([gated[j * s1 : (j + 1) * s1]] * npl, axis=0)
        mixers.append(jnp.where(chip_hot, tiled, 0.0).T)
    selh = selh.astype(BF16)

    def exchange(s):
        q = quarters[s]
        part = pl.ds(pl.multiple_of(q * feat, feat), feat)
        xs2[:, part] = dot(sel2, z2[:, part]).astype(BF16)
        copies = go(
            Copies(
                npl,
                p,
                lambda i: block(xs2, i * s1, s1, q * feat, feat),
                lambda m: block(xr, chunk + m * s1, s1, q * feat, feat),
                pdev,
                *pair(),
            )
        )
        xr[pl.ds(chunk + p * s1, s1), part] = xs2[pl.ds(p * s1, s1), part]
        return copies

    x2 = []
    for s in range(ny):
        rings[s].finish()
        x2.append(exchange(s))
        tick(rings[s + 1 : ny])

    hot_base = lambda j, i, core: (2 + j) * chunk + (core * nx + i) * s1
    hot_rings, siblings = [], []
    for j in range(COPIES):
        for s in range(ny):
            part = slice(s * feat, (s + 1) * feat)
            xr[pl.ds(hot_base(j, x, c), s1), part] = dot(selh[j * s1 : (j + 1) * s1], z2[:, part]).astype(BF16)
        hot_rings.append(
            Ring(
                nx,
                x,
                lambda i, j=j: rows(xr, hot_base(j, i, c), s1),
                lambda i, h, j=j: block(xr, hot_base(j, i, c), s1, h * (width // 2), width // 2),
                xdev,
                *pair(),
            )
        )
        siblings.append(([], *pair()))

    def to_sibling(j, i):
        items, send, recv = siblings[j]
        ref = rows(xr, hot_base(j, i, c), s1)
        item = pltpu.make_async_remote_copy(
            src_ref=ref,
            dst_ref=ref,
            send_sem=send.at[len(items)],
            recv_sem=recv.at[len(items)],
            device_id=pdev(x * CORES + 1 - c),
            device_id_type=MESH,
        )
        item.start()
        items.append(item)

    def hot_step(j):
        ring = hot_rings[j]
        k = ring.at
        ring.step()
        if k == 0:
            to_sibling(j, x)
        elif k < ring.steps:
            to_sibling(j, lax.rem(x + nx - k, nx))
            to_sibling(j, lax.rem(x + k, nx))
        else:
            to_sibling(j, lax.rem(x + k, nx))

    def hot_arrived(j):
        while hot_rings[j].at <= hot_rings[j].steps:
            hot_step(j)
        for item in siblings[j][0]:
            item.wait_recv()

    def front(i):
        part = pl.ds(i * chunk, chunk)
        acc[...] = jnp.zeros_like(acc)

        @pl.loop(0, ny)
        def _(q):
            features = pl.ds(pl.multiple_of(q * feat, feat), feat)
            a = xr[part, features]
            for half in range(2):
                acc[:, half * ff : (half + 1) * ff] += dot(a, wgu[half, features, :])

        gated = acc[:, 0:ff]
        value = gated / (1.0 + jnp.exp(-gated)) * acc[:, ff : 2 * ff]
        hid[part, pl.ds(pl.multiple_of(y * ff, ff), ff)] = value.astype(BF16)
        ref = block(hid, i * chunk, chunk, y * ff, ff)
        return go(Copies(ny, y, lambda m: ref, lambda m: block(hid, i * chunk, chunk, m * ff, ff), ydev, *pair()))

    def back(i, gathered):
        gathered.wait_recv()
        part = pl.ds(i * chunk, chunk)
        o[part, :] = dot(hid[part, :], wd[...]).astype(BF16)
        own = pl.ds(i * chunk + p * s1, s1)
        ro[own, :] = o[own, :]
        return go(
            Copies(
                npl,
                p,
                lambda m: rows(o, i * chunk + m * s1, s1),
                lambda m: rows(ro, i * chunk + m * s1, s1),
                pdev,
                *pair(),
            )
        )

    def back_hot(i, gathered):
        gathered.wait_recv()
        part = pl.ds(i * chunk, chunk)
        o[part, :] = jnp.where(own_hot, dot(hid[part, :], wd[...]), 0.0).astype(BF16)
        half = nx * s1
        away = rows(o, i * chunk + (1 - c) * half, half)
        item = pltpu.make_async_remote_copy(
            src_ref=away,
            dst_ref=rows(halves, (i - 2) * half, half),
            send_sem=half_send.at[i - 2],
            recv_sem=half_recv.at[i - 2],
            device_id=pdev(x * CORES + 1 - c),
            device_id_type=MESH,
        )
        item.start()
        siblings.append(([item], None, None))
        return item

    def back_chip(i, item):
        item.wait_recv()
        half = nx * s1
        kept = pl.ds(i * chunk + c * half, half)
        o[kept, :] += halves[pl.ds((i - 2) * half, half), :]
        own = pl.ds(i * chunk + x * s1, s1)
        ro[own, :] = o[pl.ds(i * chunk + c * half + x * s1, s1), :]
        return go(
            Copies(
                nx,
                x,
                lambda m: rows(o, i * chunk + c * half + m * s1, s1),
                lambda m: rows(ro, i * chunk + m * s1, s1),
                xdev,
                *pair(),
            )
        )

    def mixed(i, returned):
        returned.wait_recv()
        high = mixers[i].astype(BF16)
        low = (mixers[i] - high.astype(F32)).astype(BF16)
        used = nx * s1 if i > 1 else chunk
        both = jnp.concatenate([high[:, 0:used], low[:, 0:used]], axis=0)
        sums = dot(both, ro[pl.ds(i * chunk, used), :])
        return sums[0:cols] + sums[cols:]

    def deliver(b):
        copies = go(
            Copies(
                nz,
                z,
                lambda m: rows(mix, b * cols + m * tok, tok),
                lambda m: rows(inbox, b * cols + m * tok, tok),
                zdev,
                *pair(),
            )
        )
        own = pl.ds(b * cols + z * tok, tok)
        inbox[own, :] = mix[own, :]
        return copies

    def final(b, copies):
        copies.wait_recv()
        total = inbox[b * cols : b * cols + tok, :].astype(F32)
        for i in range(1, nz):
            start = b * cols + i * tok
            total += inbox[start : start + tok, :].astype(F32)
        out[b * tok : (b + 1) * tok, :] = total

    half_send, half_recv = pair()
    hot_step(0)
    hot_step(1)
    x1.wait_recv()
    y1 = go(Copies(ny, y, lambda i: mine(rows(xr, 0, chunk)), lambda m: lanes(rows(xr, 0, chunk), m, feat), ydev, *pair()))

    weights.wait()
    for copies in x2:
        copies.wait_recv()
    h1 = front(1)
    hot_step(0)
    hot_step(2)
    hot_step(1)
    hot_arrived(0)
    h2 = front(2)
    hot_step(2)
    own_out.wait()
    out_y.wait_recv()
    r1 = back(1, h1)
    y1.wait_recv()
    h0 = front(0)
    hot_arrived(1)
    h3 = front(3)
    b2 = back_hot(2, h2)
    r0 = back(0, h0)
    r2 = back_chip(2, b2)
    hot_arrived(2)
    h4 = front(4)
    blend[...] = mixed(1, r1)
    b3 = back_hot(3, h3)
    mix[0:cols, :] = mixed(0, r0).astype(BF16)
    d1 = deliver(0)
    r3 = back_chip(3, b3)
    b4 = back_hot(4, h4)
    blend[...] += mixed(2, r2)
    r4 = back_chip(4, b4)
    blend[...] += mixed(3, r3)
    mix[cols : 2 * cols, :] = (blend[...] + mixed(4, r4)).astype(BF16)
    d2 = deliver(1)
    final(0, d1)
    final(1, d2)

    for copies in started + rings + hot_rings:
        copies.wait_send()
    for items, _, _ in siblings:
        for item in items:
            item.wait_send()


def shards(
    dims, tokens_one, experts_one, gates_one, tokens_two, experts_two, gates_two, replica_pick, home, w_gate_up, w_down
):
    nz, nx, ny = dims
    npl = nx * CORES
    tok, feat = tokens_one.shape
    width = feat * ny
    ff = w_gate_up.shape[3]
    cols = nz * tok
    chunk = npl * SLOT * nz
    chunks = 2 + COPIES
    vmem = pltpu.VMEM
    dma = pltpu.SemaphoreType.DMA
    size = max(nz, npl, ny, nx) + 4
    groups = 1 + 2 + ny + 2 + 1 + 1 + 2 + ny + 2 * COPIES + 1 + 1 + 2 * chunks + 2
    any_spec = pl.BlockSpec(memory_space=pl.ANY)
    in_vmem = pl.BlockSpec(memory_space=pltpu.VMEM)
    out = pl.pallas_call(
        functools.partial(kernel, dims),
        out_shape=jax.ShapeDtypeStruct((2 * tok, feat), F32),
        in_specs=[in_vmem] * 8 + [any_spec] * 2,
        out_specs=in_vmem,
        scratch_shapes=[
            vmem((128, 128), F32),
            vmem((cols, 128), F32),
            vmem((npl * 8, 128), F32),
            vmem((cols, feat), BF16),
            vmem((cols, width), BF16),
            vmem((chunk, feat), BF16),
            vmem((chunk, width), BF16),
            vmem((chunks * chunk, width), BF16),
            vmem((chunk, 2 * ff), F32),
            vmem((chunks * chunk, ff * ny), BF16),
            vmem((chunks * chunk, feat), BF16),
            vmem((chunks * chunk, feat), BF16),
            vmem((cols, feat), F32),
            vmem((2 * cols, feat), BF16),
            vmem((2 * cols, feat), BF16),
            vmem((COPIES * nx * SLOT * nz, feat), BF16),
            vmem(w_gate_up.shape[1:], BF16),
            vmem((ff * ny, feat), BF16),
            dma((2,)),
        ]
        + [dma((size,)) for _ in range(2 * groups)],
        compiler_params=pltpu.CompilerParams(
            collective_id=0, has_side_effects=True, vmem_limit_bytes=56 * 1024 * 1024
        ),
        cost_estimate=pl.CostEstimate(flops=10_000_000_000, bytes_accessed=16_000_000, transcendentals=0),
    )(
        tokens_one,
        tokens_two,
        experts_one.T,
        gates_one.T,
        experts_two.T,
        gates_two.T,
        replica_pick.T,
        home[None, :],
        w_gate_up,
        w_down,
    )
    return out[:tok].astype(BF16), out[tok:].astype(BF16)


def solution(mesh):
    placed = (
        P("expert", "inner"),
        P("expert", None),
        P("expert", None),
        P("expert", "inner"),
        P("expert", None),
        P("expert", None),
        P("expert", None),
        P(),
        P("expert", None, None, "inner"),
        P("expert", "inner", None),
    )
    experts, inner = mesh.shape["expert"], mesh.shape["inner"]
    nx = 4 if experts >= 16 else 2
    dims = (experts // (nx * CORES), nx, inner)
    return jax.shard_map(
        functools.partial(shards, dims),
        mesh=mesh,
        in_specs=placed,
        out_specs=(P("expert", "inner"), P("expert", "inner")),
        check_vma=False,
    )
```

```python
import functools

import jax
import jax.numpy as jnp
from jax import lax
from jax.experimental import pallas as pl
from jax.experimental.pallas import tpu as pltpu
from jax.sharding import PartitionSpec as P

MESH = pl.DeviceIdType.MESH
TOPK = 8
COPIES = 3
SLOT = 2
CORES = 2
F32 = jnp.float32
BF16 = jnp.bfloat16
E1, G1, E2, G2, PICK = 0, 8, 16, 24, 32


def dot(a, b):
    return jnp.dot(a, b, preferred_element_type=F32)


def iota(shape, dim):
    return lax.broadcasted_iota(jnp.int32, shape, dim)


class Copies:
    def __init__(self, n, me, src, dst, device, send, recv):
        self.items = []
        for i in range(1, n):
            peer = lax.rem(me + i, n)
            self.items.append(
                pltpu.make_async_remote_copy(
                    src_ref=src(peer),
                    dst_ref=dst(me),
                    send_sem=send.at[i],
                    recv_sem=recv.at[i],
                    device_id=device(peer),
                    device_id_type=MESH,
                )
            )

    def start(self):
        for item in self.items:
            item.start()

    def wait_from(self, ahead):
        self.items[len(self.items) - ahead].wait_recv()

    def wait_recv(self):
        for item in self.items:
            item.wait_recv()

    def wait_send(self):
        for item in self.items:
            item.wait_send()


class Ring:
    def __init__(self, n, me, block, half, device, send, recv):
        self.steps = n // 2
        self.at = 0
        self.pairs = []
        right, left = lax.rem(me + 1, n), lax.rem(me + n - 1, n)
        for k in range(1, self.steps + 1):
            pair = []
            for way, (target, index) in enumerate(
                ((right, lax.rem(me + n - (k - 1), n)), (left, lax.rem(me + (k - 1), n)))
            ):
                ref = half(index, way) if k == self.steps else block(index)
                pair.append(
                    pltpu.make_async_remote_copy(
                        src_ref=ref,
                        dst_ref=ref,
                        send_sem=send.at[2 * k + way],
                        recv_sem=recv.at[2 * k + way],
                        device_id=device(target),
                        device_id_type=MESH,
                    )
                )
            self.pairs.append(pair)

    def step(self):
        if self.at > self.steps:
            return
        if self.at > 0:
            for item in self.pairs[self.at - 1]:
                item.wait_recv()
        if self.at < self.steps:
            for item in self.pairs[self.at]:
                item.start()
        self.at += 1

    def finish(self):
        while self.at <= self.steps:
            self.step()

    def wait_send(self):
        for pair in self.pairs:
            for item in pair:
                item.wait_send()


def kernel(
    dims,
    tok1,
    tok2,
    e1,
    g1,
    e2,
    g2,
    picks,
    home,
    w_in,
    w_out,
    out,
    pack,
    info,
    counts,
    z1,
    z2,
    xs1,
    xs2,
    xr,
    acc,
    hid,
    o,
    ro,
    blend,
    mix,
    inbox,
    halves,
    wgu,
    wd,
    local,
    *sems,
):
    nz, nx, ny = dims
    npl = nx * CORES
    tok, feat = tok1.shape
    width = feat * ny
    ff = w_in.shape[3]
    cols = nz * tok
    s1 = SLOT * nz
    chunk = npl * s1
    sems = list(sems)

    e = lax.axis_index("expert")
    y = lax.axis_index("inner")
    z = e // npl
    p = lax.rem(e, npl)
    x = p // CORES
    c = lax.rem(p, CORES)
    zdev = lambda other: (other * npl + p, y)
    pdev = lambda other: (z * npl + other, y)
    ydev = lambda other: (e, other)
    xdev = lambda other: (z * npl + other * CORES + c, y)

    def pair():
        return sems.pop(0), sems.pop(0)

    def rows(ref, start, size):
        return ref.at[pl.ds(start, size)]

    def lanes(ref, index, size):
        return ref.at[:, pl.ds(pl.multiple_of(index * size, size), size)]

    def block(ref, r, rs, l, ls):
        return ref.at[pl.ds(r, rs), pl.ds(pl.multiple_of(l, ls), ls)]

    weights = pltpu.make_async_copy(w_in.at[0], wgu, local.at[0])
    weights.start()
    own_out = pltpu.make_async_copy(lanes(w_out.at[0], y, feat), rows(wd, y * ff, ff), local.at[1])
    own_out.start()

    pack[...] = jnp.zeros_like(pack)
    pack[E1 : E1 + TOPK, 0:tok] = e1[...].astype(F32)
    pack[G1 : G1 + TOPK, 0:tok] = g1[...]
    pack[E2 : E2 + TOPK, 0:tok] = e2[...].astype(F32)
    pack[G2 : G2 + TOPK, 0:tok] = g2[...]
    pack[PICK : PICK + TOPK, 0:tok] = lax.rem(picks[...], COPIES + 1).astype(F32)
    info[pl.ds(z * tok, tok), :] = pack[...].T[0:tok, :]
    z1[pl.ds(z * tok, tok), :] = tok1[...]
    z2[pl.ds(z * tok, tok), pl.ds(pl.multiple_of(y * feat, feat), feat)] = tok2[...]

    barrier = pltpu.get_barrier_semaphore()
    for i in range(1, nz):
        pl.semaphore_signal(barrier, inc=1, device_id=zdev(lax.rem(z + i, nz)), device_id_type=MESH)
    for i in range(1, npl):
        pl.semaphore_signal(barrier, inc=1, device_id=pdev(lax.rem(p + i, npl)), device_id_type=MESH)
    for i in range(1, ny):
        pl.semaphore_signal(barrier, inc=1, device_id=ydev(lax.rem(y + i, ny)), device_id_type=MESH)

    shape = (cols, cols)
    earlier = ((iota(shape, 0) // tok == iota(shape, 1) // tok) & (iota(shape, 0) < iota(shape, 1))).astype(BF16)
    here = home.shape[1]
    held = home[0:1, :] == z * npl + iota((chunk, here), 0) // s1
    holder = jnp.sum(jnp.where(held, iota((chunk, here), 1).astype(F32), 0.0), axis=1, keepdims=True)

    pl.semaphore_wait(barrier, nz + npl + ny - 3)

    started = []

    def go(copies):
        copies.start()
        started.append(copies)
        return copies

    order = [0, 1, 3, 2] if ny == 4 else list(range(ny))
    quarters = [lax.rem(y + s, ny) for s in order]
    rings = [
        Ring(
            nz,
            z,
            lambda i, q=q: block(z2, i * tok, tok, q * feat, feat),
            lambda i, h, q=q: block(z2, i * tok, tok, q * feat + h * (feat // 2), feat // 2),
            zdev,
            *pair(),
        )
        for q in quarters
    ]
    rings.append(
        Ring(
            nz,
            z,
            lambda i: rows(z1, i * tok, tok),
            lambda i, h: block(z1, i * tok, tok, h * (feat // 2), feat // 2),
            zdev,
            *pair(),
        )
    )
    tok2_y = go(Copies(ny, y, lambda i: tok2, lambda m: lanes(rows(z2, z * tok, tok), m, feat), ydev, *pair()))
    rings[0].step()
    rings[ny].step()
    info_z = go(
        Copies(nz, z, lambda i: rows(info, z * tok, tok), lambda m: rows(info, m * tok, tok), zdev, *pair())
    )

    def tick(some):
        for ring in some:
            ring.step()

    tok2_y.wait_recv()
    tick(rings[1:ny])
    out_y = go(
        Copies(ny, y, lambda i: lanes(w_out.at[0], i, feat), lambda m: rows(wd, m * ff, ff), ydev, *pair())
    )

    info_z.wait_recv()
    every = info[...]
    turned = every.T
    field = lambda base, k: turned[base + k : base + k + 1, :]
    expert_lane = iota((cols, 128), 1).astype(F32)
    tally = jnp.zeros((cols, 128), F32)
    for k in range(TOPK):
        tally += (every[:, E1 + k : E1 + k + 1] == expert_lane).astype(F32)
    counts[pl.ds(p * 8, 8), :] = jnp.broadcast_to(jnp.sum(tally, axis=0, keepdims=True), (8, 128))
    counts_p = go(
        Copies(npl, p, lambda i: rows(counts, p * 8, 8), lambda m: rows(counts, m * 8, 8), pdev, *pair())
    )
    tick([rings[0], rings[ny]])

    def selection(match, length):
        number = dot(match.astype(BF16), earlier)
        slot = (iota((length, cols), 0) // nz % SLOT).astype(F32)
        return jnp.where(number == slot, match, 0.0)

    def sourced(length):
        return (iota((length, cols), 0) % nz) == (iota((length, cols), 1) // tok)

    same_z = sourced(chunk)
    match = jnp.zeros((chunk, cols), F32)
    gate = jnp.zeros((chunk, cols), F32)
    for k in range(TOPK):
        hit = (field(E1, k) == holder) & same_z
        match += hit.astype(F32)
        gate += jnp.where(hit, field(G1, k), 0.0)
    sel1 = selection(match, chunk)
    mixers = [(sel1 * gate).T]
    sel1 = sel1.astype(BF16)
    tick(rings)
    counts_p.wait_recv()
    total = counts[0:8, :]
    for other in range(1, npl):
        total += counts[other * 8 : other * 8 + 8, :]
    lane = iota((1, 128), 1)
    total = jnp.where(lane < nz * npl, total[0:1, :], -1.0)
    most = jnp.max(total, axis=1, keepdims=True)
    hot = jnp.min(jnp.where(total == most, lane.astype(F32), 1e6), axis=1, keepdims=True)

    match = jnp.zeros((chunk, cols), F32)
    gate = jnp.zeros((chunk, cols), F32)
    for k in range(TOPK):
        chosen, pick = field(E2, k), field(PICK, k)
        hit = (chosen == holder) & ((chosen != hot) | (pick == 0.0)) & same_z
        match += hit.astype(F32)
        gate += jnp.where(hit, field(G2, k), 0.0)
    sel2 = selection(match, chunk)
    mixer2 = (sel2 * gate).T
    sel2 = sel2.astype(BF16)
    tick(rings)

    rings[ny].finish()
    xs1[...] = dot(sel1, z1[...]).astype(BF16)
    mine = lambda ref: lanes(ref, y, feat)
    x1 = go(
        Copies(npl, p, lambda i: rows(xs1, i * s1, s1), lambda m: mine(rows(xr, m * s1, s1)), pdev, *pair())
    )
    xr[pl.ds(p * s1, s1), pl.ds(pl.multiple_of(y * feat, feat), feat)] = xs1[pl.ds(p * s1, s1), :]
    tick(rings[1:ny])

    hots = COPIES * s1
    copy_number = (iota((hots, cols), 0) // s1 + 1).astype(F32)
    same_copy = sourced(hots)
    match = jnp.zeros((hots, cols), F32)
    gate = jnp.zeros((hots, cols), F32)
    for k in range(TOPK):
        hit = (field(E2, k) == hot) & (field(PICK, k) == copy_number) & same_copy
        match += hit.astype(F32)
        gate += jnp.where(hit, field(G2, k), 0.0)
    selh = selection(match, hots)
    gated = selh * gate
    chip = z * nx + iota((chunk, here), 0) // s1
    on_chip = (home[0:1, :] // CORES == chip) & (iota((chunk, here), 0) < nx * s1)
    total = jnp.where(on_chip & (iota((chunk, here), 1).astype(F32) == hot), 1.0, 0.0)
    chip_hot = jnp.sum(total, axis=1, keepdims=True) > 0.0
    own = jnp.where((home[0:1, :] == e) & (iota((1, here), 1).astype(F32) == hot), 1.0, 0.0)
    own_hot = jnp.sum(own, axis=1, keepdims=True) > 0.0
    mixers.append(mixer2)
    for j in range(COPIES):
        tiled = jnp.concatenate([gated[j * s1 : (j + 1) * s1]] * npl, axis=0)
        mixers.append(jnp.where(chip_hot, tiled, 0.0).T)
    selh = selh.astype(BF16)

    def exchange(s):
        q = quarters[s]
        part = pl.ds(pl.multiple_of(q * feat, feat), feat)
        xs2[:, part] = dot(sel2, z2[:, part]).astype(BF16)
        copies = go(
            Copies(
                npl,
                p,
                lambda i: block(xs2, i * s1, s1, q * feat, feat),
                lambda m: block(xr, chunk + m * s1, s1, q * feat, feat),
                pdev,
                *pair(),
            )
        )
        xr[pl.ds(chunk + p * s1, s1), part] = xs2[pl.ds(p * s1, s1), part]
        return copies

    x2 = []
    for s in range(ny):
        rings[s].finish()
        x2.append(exchange(s))
        tick(rings[s + 1 : ny])

    hot_base = lambda j, i, core: (2 + j) * chunk + (core * nx + i) * s1
    hot_rings, siblings = [], []
    for j in range(COPIES):
        for s in range(ny):
            part = slice(s * feat, (s + 1) * feat)
            xr[pl.ds(hot_base(j, x, c), s1), part] = dot(selh[j * s1 : (j + 1) * s1], z2[:, part]).astype(BF16)
        hot_rings.append(
            Ring(
                nx,
                x,
                lambda i, j=j: rows(xr, hot_base(j, i, c), s1),
                lambda i, h, j=j: block(xr, hot_base(j, i, c), s1, h * (width // 2), width // 2),
                xdev,
                *pair(),
            )
        )
        siblings.append(([], *pair()))

    def to_sibling(j, i):
        items, send, recv = siblings[j]
        ref = rows(xr, hot_base(j, i, c), s1)
        item = pltpu.make_async_remote_copy(
            src_ref=ref,
            dst_ref=ref,
            send_sem=send.at[len(items)],
            recv_sem=recv.at[len(items)],
            device_id=pdev(x * CORES + 1 - c),
            device_id_type=MESH,
        )
        item.start()
        items.append(item)

    def hot_step(j):
        ring = hot_rings[j]
        k = ring.at
        ring.step()
        if k == 0:
            to_sibling(j, x)
        elif k < ring.steps:
            to_sibling(j, lax.rem(x + nx - k, nx))
            to_sibling(j, lax.rem(x + k, nx))
        else:
            to_sibling(j, lax.rem(x + k, nx))

    def hot_arrived(j):
        while hot_rings[j].at <= hot_rings[j].steps:
            hot_step(j)
        for item in siblings[j][0]:
            item.wait_recv()

    def front(i):
        part = pl.ds(i * chunk, chunk)
        acc[...] = jnp.zeros_like(acc)

        @pl.loop(0, ny)
        def _(q):
            features = pl.ds(pl.multiple_of(q * feat, feat), feat)
            a = xr[part, features]
            for half in range(2):
                acc[:, half * ff : (half + 1) * ff] += dot(a, wgu[half, features, :])

        gated = acc[:, 0:ff]
        value = gated / (1.0 + jnp.exp(-gated)) * acc[:, ff : 2 * ff]
        hid[part, pl.ds(pl.multiple_of(y * ff, ff), ff)] = value.astype(BF16)
        ref = block(hid, i * chunk, chunk, y * ff, ff)
        return go(Copies(ny, y, lambda m: ref, lambda m: block(hid, i * chunk, chunk, m * ff, ff), ydev, *pair()))

    def back(i, gathered):
        gathered.wait_recv()
        part = pl.ds(i * chunk, chunk)
        o[part, :] = dot(hid[part, :], wd[...]).astype(BF16)
        own = pl.ds(i * chunk + p * s1, s1)
        ro[own, :] = o[own, :]
        return go(
            Copies(
                npl,
                p,
                lambda m: rows(o, i * chunk + m * s1, s1),
                lambda m: rows(ro, i * chunk + m * s1, s1),
                pdev,
                *pair(),
            )
        )

    def back_hot(i, gathered):
        gathered.wait_recv()
        part = pl.ds(i * chunk, chunk)
        o[part, :] = jnp.where(own_hot, dot(hid[part, :], wd[...]), 0.0).astype(BF16)
        half = nx * s1
        away = rows(o, i * chunk + (1 - c) * half, half)
        item = pltpu.make_async_remote_copy(
            src_ref=away,
            dst_ref=rows(halves, (i - 2) * half, half),
            send_sem=half_send.at[i - 2],
            recv_sem=half_recv.at[i - 2],
            device_id=pdev(x * CORES + 1 - c),
            device_id_type=MESH,
        )
        item.start()
        siblings.append(([item], None, None))
        return item

    def back_chip(i, item):
        item.wait_recv()
        half = nx * s1
        kept = pl.ds(i * chunk + c * half, half)
        o[kept, :] += halves[pl.ds((i - 2) * half, half), :]
        own = pl.ds(i * chunk + x * s1, s1)
        ro[own, :] = o[pl.ds(i * chunk + c * half + x * s1, s1), :]
        return go(
            Copies(
                nx,
                x,
                lambda m: rows(o, i * chunk + c * half + m * s1, s1),
                lambda m: rows(ro, i * chunk + m * s1, s1),
                xdev,
                *pair(),
            )
        )

    def mixed(i, returned):
        returned.wait_recv()
        high = mixers[i].astype(BF16)
        low = (mixers[i] - high.astype(F32)).astype(BF16)
        used = nx * s1 if i > 1 else chunk
        both = jnp.concatenate([high[:, 0:used], low[:, 0:used]], axis=0)
        sums = dot(both, ro[pl.ds(i * chunk, used), :])
        return sums[0:cols] + sums[cols:]

    def block_for(b, ahead):
        return pl.ds(b * cols + lax.rem(z + ahead + nz, nz) * tok, tok)

    def slot(b, k):
        return pl.ds(b * cols + k * tok, tok)

    class Sums:
        def __init__(self, b):
            self.b = b
            self.sems = pair()
            self.items = []
            inbox[slot(b, 0), :] = mix[block_for(b, 0), :]
            whole, low, high = pl.ds(0, feat), pl.ds(0, feat // 2), pl.ds(feat // 2, feat // 2)
            if nz == 8:
                self.send(-1, -1, 1, whole)
                self.send(1, 1, 2, whole)
                self.send(-1, -3, 5, whole)
                self.send(1, 3, 6, whole)
                self.send(-2, -4, 7, low)
                self.send(2, 4, 7, high)
            else:
                for i in range(1, nz):
                    self.send(i, i, i, whole)

        def send(self, step, ahead, k, part):
            i = len(self.items)
            send, recv = self.sems
            item = pltpu.make_async_remote_copy(
                src_ref=mix.at[block_for(self.b, ahead), part],
                dst_ref=inbox.at[slot(self.b, k), part],
                send_sem=send.at[i],
                recv_sem=recv.at[i],
                device_id=zdev(lax.rem(z + step + nz, nz)),
                device_id_type=MESH,
            )
            item.start()
            self.items.append(item)

        def relay(self):
            if nz != 8:
                return
            for item in self.items[2:6]:
                item.wait_recv()
            b, half = self.b, feat // 2
            for ahead, k in ((-2, 5), (2, 6)):
                total = mix[block_for(b, ahead), :].astype(F32) + inbox[slot(b, k), :].astype(F32)
                opposite = inbox[slot(b, 7), :].astype(F32)
                nearer = iota((tok, feat), 1) < half if ahead < 0 else iota((tok, feat), 1) >= half
                mix[block_for(b, ahead), :] = (total + jnp.where(nearer, opposite, 0.0)).astype(BF16)
            whole = pl.ds(0, feat)
            self.send(-2, -2, 3, whole)
            self.send(2, 2, 4, whole)

        def finish(self):
            b = self.b
            if nz == 8:
                for item in self.items[:2] + self.items[6:]:
                    item.wait_recv()
            else:
                for item in self.items:
                    item.wait_recv()
            total = inbox[slot(b, 0), :].astype(F32)
            for k in range(1, 5 if nz == 8 else nz):
                total += inbox[slot(b, k), :].astype(F32)
            out[b * tok : (b + 1) * tok, :] = total

        def wait_send(self):
            for item in self.items:
                item.wait_send()

    half_send, half_recv = pair()
    hot_step(0)
    hot_step(1)
    x1.wait_recv()
    y1 = go(Copies(ny, y, lambda i: mine(rows(xr, 0, chunk)), lambda m: lanes(rows(xr, 0, chunk), m, feat), ydev, *pair()))

    weights.wait()
    for copies in x2:
        copies.wait_recv()
    h1 = front(1)
    hot_step(0)
    hot_step(2)
    hot_step(1)
    hot_arrived(0)
    h2 = front(2)
    hot_step(2)
    own_out.wait()
    out_y.wait_recv()
    r1 = back(1, h1)
    y1.wait_recv()
    h0 = front(0)
    hot_arrived(1)
    h3 = front(3)
    b2 = back_hot(2, h2)
    r0 = back(0, h0)
    r2 = back_chip(2, b2)
    hot_arrived(2)
    h4 = front(4)
    blend[...] = mixed(1, r1)
    b3 = back_hot(3, h3)
    mix[0:cols, :] = mixed(0, r0).astype(BF16)
    d1 = Sums(0)
    r3 = back_chip(3, b3)
    b4 = back_hot(4, h4)
    blend[...] += mixed(2, r2)
    r4 = back_chip(4, b4)
    blend[...] += mixed(3, r3)
    d1.relay()
    mix[cols : 2 * cols, :] = (blend[...] + mixed(4, r4)).astype(BF16)
    d2 = Sums(1)
    d2.relay()
    d1.finish()
    d2.finish()

    for copies in started + rings + hot_rings + [d1, d2]:
        copies.wait_send()
    for items, _, _ in siblings:
        for item in items:
            item.wait_send()


def shards(
    dims, tokens_one, experts_one, gates_one, tokens_two, experts_two, gates_two, replica_pick, home, w_gate_up, w_down
):
    nz, nx, ny = dims
    npl = nx * CORES
    tok, feat = tokens_one.shape
    width = feat * ny
    ff = w_gate_up.shape[3]
    cols = nz * tok
    chunk = npl * SLOT * nz
    chunks = 2 + COPIES
    vmem = pltpu.VMEM
    dma = pltpu.SemaphoreType.DMA
    size = max(nz, npl, ny, nx) + 4
    groups = 1 + 2 + ny + 2 + 1 + 1 + 2 + ny + 2 * COPIES + 1 + 1 + 2 * chunks + 2
    any_spec = pl.BlockSpec(memory_space=pl.ANY)
    in_vmem = pl.BlockSpec(memory_space=pltpu.VMEM)
    out = pl.pallas_call(
        functools.partial(kernel, dims),
        out_shape=jax.ShapeDtypeStruct((2 * tok, feat), F32),
        in_specs=[in_vmem] * 8 + [any_spec] * 2,
        out_specs=in_vmem,
        scratch_shapes=[
            vmem((128, 128), F32),
            vmem((cols, 128), F32),
            vmem((npl * 8, 128), F32),
            vmem((cols, feat), BF16),
            vmem((cols, width), BF16),
            vmem((chunk, feat), BF16),
            vmem((chunk, width), BF16),
            vmem((chunks * chunk, width), BF16),
            vmem((chunk, 2 * ff), F32),
            vmem((chunks * chunk, ff * ny), BF16),
            vmem((chunks * chunk, feat), BF16),
            vmem((chunks * chunk, feat), BF16),
            vmem((cols, feat), F32),
            vmem((2 * cols, feat), BF16),
            vmem((2 * cols, feat), BF16),
            vmem((COPIES * nx * SLOT * nz, feat), BF16),
            vmem(w_gate_up.shape[1:], BF16),
            vmem((ff * ny, feat), BF16),
            dma((2,)),
        ]
        + [dma((size,)) for _ in range(2 * groups)],
        compiler_params=pltpu.CompilerParams(
            collective_id=0, has_side_effects=True, vmem_limit_bytes=56 * 1024 * 1024
        ),
        cost_estimate=pl.CostEstimate(flops=10_000_000_000, bytes_accessed=16_000_000, transcendentals=0),
    )(
        tokens_one,
        tokens_two,
        experts_one.T,
        gates_one.T,
        experts_two.T,
        gates_two.T,
        replica_pick.T,
        home[None, :],
        w_gate_up,
        w_down,
    )
    return out[:tok].astype(BF16), out[tok:].astype(BF16)


def solution(mesh):
    placed = (
        P("expert", "inner"),
        P("expert", None),
        P("expert", None),
        P("expert", "inner"),
        P("expert", None),
        P("expert", None),
        P("expert", None),
        P(),
        P("expert", None, None, "inner"),
        P("expert", "inner", None),
    )
    experts, inner = mesh.shape["expert"], mesh.shape["inner"]
    nx = 4 if experts >= 16 else 2
    dims = (experts // (nx * CORES), nx, inner)
    return jax.shard_map(
        functools.partial(shards, dims),
        mesh=mesh,
        in_specs=placed,
        out_specs=(P("expert", "inner"), P("expert", "inner")),
        check_vma=False,
    )
```

```python
import functools

import jax
import jax.numpy as jnp
from jax import lax
from jax.experimental import pallas as pl
from jax.experimental.pallas import tpu as pltpu
from jax.sharding import PartitionSpec as P

MESH = pl.DeviceIdType.MESH
TOPK = 8
COPIES = 3
SLOT = 2
CORES = 2
F32 = jnp.float32
BF16 = jnp.bfloat16
E1, G1, E2, G2, PICK = 0, 8, 16, 24, 32


def dot(a, b):
    return jnp.dot(a, b, preferred_element_type=F32)


def iota(shape, dim):
    return lax.broadcasted_iota(jnp.int32, shape, dim)


class Copies:
    def __init__(self, n, me, src, dst, device, send, recv):
        self.items = []
        for i in range(1, n):
            peer = lax.rem(me + i, n)
            self.items.append(
                pltpu.make_async_remote_copy(
                    src_ref=src(peer),
                    dst_ref=dst(me),
                    send_sem=send.at[i],
                    recv_sem=recv.at[i],
                    device_id=device(peer),
                    device_id_type=MESH,
                )
            )

    def start(self):
        for item in self.items:
            item.start()

    def wait_from(self, ahead):
        self.items[len(self.items) - ahead].wait_recv()

    def wait_recv(self):
        for item in self.items:
            item.wait_recv()

    def wait_send(self):
        for item in self.items:
            item.wait_send()


class Ring:
    def __init__(self, n, me, block, half, device, send, recv):
        self.steps = n // 2
        self.at = 0
        self.pairs = []
        right, left = lax.rem(me + 1, n), lax.rem(me + n - 1, n)
        for k in range(1, self.steps + 1):
            pair = []
            for way, (target, index) in enumerate(
                ((right, lax.rem(me + n - (k - 1), n)), (left, lax.rem(me + (k - 1), n)))
            ):
                ref = half(index, way) if k == self.steps else block(index)
                pair.append(
                    pltpu.make_async_remote_copy(
                        src_ref=ref,
                        dst_ref=ref,
                        send_sem=send.at[2 * k + way],
                        recv_sem=recv.at[2 * k + way],
                        device_id=device(target),
                        device_id_type=MESH,
                    )
                )
            self.pairs.append(pair)

    def step(self):
        if self.at > self.steps:
            return
        if self.at > 0:
            for item in self.pairs[self.at - 1]:
                item.wait_recv()
        if self.at < self.steps:
            for item in self.pairs[self.at]:
                item.start()
        self.at += 1

    def finish(self):
        while self.at <= self.steps:
            self.step()

    def wait_send(self):
        for pair in self.pairs:
            for item in pair:
                item.wait_send()


def kernel(
    dims,
    tok1,
    tok2,
    e1,
    g1,
    e2,
    g2,
    picks,
    home,
    w_in,
    w_out,
    out,
    pack,
    info,
    counts,
    z1,
    z2,
    xs1,
    xs2,
    xr,
    acc,
    hid,
    o,
    ro,
    blend,
    mix,
    inbox,
    halves,
    wgu,
    wd,
    local,
    *sems,
):
    nz, nx, ny = dims
    npl = nx * CORES
    tok, feat = tok1.shape
    width = feat * ny
    ff = w_in.shape[3]
    cols = nz * tok
    s1 = SLOT * nz
    chunk = npl * s1
    sems = list(sems)

    e = lax.axis_index("expert")
    y = lax.axis_index("inner")
    z = e // npl
    p = lax.rem(e, npl)
    x = p // CORES
    c = lax.rem(p, CORES)
    zdev = lambda other: (other * npl + p, y)
    pdev = lambda other: (z * npl + other, y)
    ydev = lambda other: (e, other)
    xdev = lambda other: (z * npl + other * CORES + c, y)

    def pair():
        return sems.pop(0), sems.pop(0)

    def rows(ref, start, size):
        return ref.at[pl.ds(start, size)]

    def lanes(ref, index, size):
        return ref.at[:, pl.ds(pl.multiple_of(index * size, size), size)]

    def block(ref, r, rs, l, ls):
        return ref.at[pl.ds(r, rs), pl.ds(pl.multiple_of(l, ls), ls)]

    weights = pltpu.make_async_copy(w_in.at[0], wgu, local.at[0])
    weights.start()
    own_out = pltpu.make_async_copy(lanes(w_out.at[0], y, feat), rows(wd, y * ff, ff), local.at[1])
    own_out.start()

    pack[...] = jnp.zeros_like(pack)
    pack[E1 : E1 + TOPK, 0:tok] = e1[...].astype(F32)
    pack[G1 : G1 + TOPK, 0:tok] = g1[...]
    pack[E2 : E2 + TOPK, 0:tok] = e2[...].astype(F32)
    pack[G2 : G2 + TOPK, 0:tok] = g2[...]
    pack[PICK : PICK + TOPK, 0:tok] = lax.rem(picks[...], COPIES + 1).astype(F32)
    info[pl.ds(z * tok, tok), :] = pack[...].T[0:tok, :]
    z1[pl.ds(z * tok, tok), :] = tok1[...]
    z2[pl.ds(z * tok, tok), pl.ds(pl.multiple_of(y * feat, feat), feat)] = tok2[...]

    barrier = pltpu.get_barrier_semaphore()
    for i in range(1, nz):
        pl.semaphore_signal(barrier, inc=1, device_id=zdev(lax.rem(z + i, nz)), device_id_type=MESH)
    for i in range(1, npl):
        pl.semaphore_signal(barrier, inc=1, device_id=pdev(lax.rem(p + i, npl)), device_id_type=MESH)
    for i in range(1, ny):
        pl.semaphore_signal(barrier, inc=1, device_id=ydev(lax.rem(y + i, ny)), device_id_type=MESH)

    shape = (cols, cols)
    earlier = ((iota(shape, 0) // tok == iota(shape, 1) // tok) & (iota(shape, 0) < iota(shape, 1))).astype(BF16)
    here = home.shape[1]
    held = home[0:1, :] == z * npl + iota((chunk, here), 0) // s1
    holder = jnp.sum(jnp.where(held, iota((chunk, here), 1).astype(F32), 0.0), axis=1, keepdims=True)

    pl.semaphore_wait(barrier, nz + npl + ny - 3)

    started = []

    def go(copies):
        copies.start()
        started.append(copies)
        return copies

    order = [0, 1, 3, 2] if ny == 4 else list(range(ny))
    quarters = [lax.rem(y + s, ny) for s in order]
    rings = [
        Ring(
            nz,
            z,
            lambda i, q=q: block(z2, i * tok, tok, q * feat, feat),
            lambda i, h, q=q: block(z2, i * tok, tok, q * feat + h * (feat // 2), feat // 2),
            zdev,
            *pair(),
        )
        for q in quarters
    ]
    rings.append(
        Ring(
            nz,
            z,
            lambda i: rows(z1, i * tok, tok),
            lambda i, h: block(z1, i * tok, tok, h * (feat // 2), feat // 2),
            zdev,
            *pair(),
        )
    )
    tok2_y = go(Copies(ny, y, lambda i: tok2, lambda m: lanes(rows(z2, z * tok, tok), m, feat), ydev, *pair()))
    rings[0].step()
    rings[ny].step()
    info_z = go(
        Copies(nz, z, lambda i: rows(info, z * tok, tok), lambda m: rows(info, m * tok, tok), zdev, *pair())
    )

    def tick(some):
        for ring in some:
            ring.step()

    tok2_y.wait_recv()
    tick(rings[1:ny])
    out_y = go(
        Copies(ny, y, lambda i: lanes(w_out.at[0], i, feat), lambda m: rows(wd, m * ff, ff), ydev, *pair())
    )

    info_z.wait_recv()
    every = info[...]
    turned = every.T
    field = lambda base, k: turned[base + k : base + k + 1, :]
    expert_lane = iota((cols, 128), 1).astype(F32)
    tally = jnp.zeros((cols, 128), F32)
    for k in range(TOPK):
        tally += (every[:, E1 + k : E1 + k + 1] == expert_lane).astype(F32)
    counts[pl.ds(p * 8, 8), :] = jnp.broadcast_to(jnp.sum(tally, axis=0, keepdims=True), (8, 128))
    counts_p = go(
        Copies(npl, p, lambda i: rows(counts, p * 8, 8), lambda m: rows(counts, m * 8, 8), pdev, *pair())
    )
    tick([rings[0], rings[ny]])

    def selection(match, length):
        number = dot(match.astype(BF16), earlier)
        slot = (iota((length, cols), 0) // nz % SLOT).astype(F32)
        return jnp.where(number == slot, match, 0.0)

    def sourced(length):
        return (iota((length, cols), 0) % nz) == (iota((length, cols), 1) // tok)

    same_z = sourced(chunk)
    match = jnp.zeros((chunk, cols), F32)
    gate = jnp.zeros((chunk, cols), F32)
    for k in range(TOPK):
        hit = (field(E1, k) == holder) & same_z
        match += hit.astype(F32)
        gate += jnp.where(hit, field(G1, k), 0.0)
    sel1 = selection(match, chunk)
    mixers = [(sel1 * gate).T]
    sel1 = sel1.astype(BF16)
    tick(rings)
    counts_p.wait_recv()
    total = counts[0:8, :]
    for other in range(1, npl):
        total += counts[other * 8 : other * 8 + 8, :]
    lane = iota((1, 128), 1)
    total = jnp.where(lane < nz * npl, total[0:1, :], -1.0)
    most = jnp.max(total, axis=1, keepdims=True)
    hot = jnp.min(jnp.where(total == most, lane.astype(F32), 1e6), axis=1, keepdims=True)

    match = jnp.zeros((chunk, cols), F32)
    gate = jnp.zeros((chunk, cols), F32)
    for k in range(TOPK):
        chosen, pick = field(E2, k), field(PICK, k)
        hit = (chosen == holder) & ((chosen != hot) | (pick == 0.0)) & same_z
        match += hit.astype(F32)
        gate += jnp.where(hit, field(G2, k), 0.0)
    sel2 = selection(match, chunk)
    mixer2 = (sel2 * gate).T
    sel2 = sel2.astype(BF16)
    tick(rings)

    rings[ny].finish()
    xs1[...] = dot(sel1, z1[...]).astype(BF16)
    mine = lambda ref: lanes(ref, y, feat)
    x1 = go(
        Copies(npl, p, lambda i: rows(xs1, i * s1, s1), lambda m: mine(rows(xr, m * s1, s1)), pdev, *pair())
    )
    xr[pl.ds(p * s1, s1), pl.ds(pl.multiple_of(y * feat, feat), feat)] = xs1[pl.ds(p * s1, s1), :]
    tick(rings[1:ny])

    hots = COPIES * s1
    copy_number = (iota((hots, cols), 0) // s1 + 1).astype(F32)
    same_copy = sourced(hots)
    match = jnp.zeros((hots, cols), F32)
    gate = jnp.zeros((hots, cols), F32)
    for k in range(TOPK):
        hit = (field(E2, k) == hot) & (field(PICK, k) == copy_number) & same_copy
        match += hit.astype(F32)
        gate += jnp.where(hit, field(G2, k), 0.0)
    selh = selection(match, hots)
    gated = selh * gate
    chip = z * nx + iota((chunk, here), 0) // s1
    on_chip = (home[0:1, :] // CORES == chip) & (iota((chunk, here), 0) < nx * s1)
    total = jnp.where(on_chip & (iota((chunk, here), 1).astype(F32) == hot), 1.0, 0.0)
    chip_hot = jnp.sum(total, axis=1, keepdims=True) > 0.0
    own = jnp.where((home[0:1, :] == e) & (iota((1, here), 1).astype(F32) == hot), 1.0, 0.0)
    own_hot = jnp.sum(own, axis=1, keepdims=True) > 0.0
    mixers.append(mixer2)
    for j in range(COPIES):
        tiled = jnp.concatenate([gated[j * s1 : (j + 1) * s1]] * npl, axis=0)
        mixers.append(jnp.where(chip_hot, tiled, 0.0).T)
    selh = selh.astype(BF16)

    def exchange(s):
        q = quarters[s]
        part = pl.ds(pl.multiple_of(q * feat, feat), feat)
        xs2[:, part] = dot(sel2, z2[:, part]).astype(BF16)
        copies = go(
            Copies(
                npl,
                p,
                lambda i: block(xs2, i * s1, s1, q * feat, feat),
                lambda m: block(xr, chunk + m * s1, s1, q * feat, feat),
                pdev,
                *pair(),
            )
        )
        xr[pl.ds(chunk + p * s1, s1), part] = xs2[pl.ds(p * s1, s1), part]
        return copies

    x2 = []
    for s in range(ny):
        rings[s].finish()
        x2.append(exchange(s))
        tick(rings[s + 1 : ny])

    hot_base = lambda j, i, core: (2 + j) * chunk + (core * nx + i) * s1
    hot_rings, siblings = [], []
    for j in range(COPIES):
        for s in range(ny):
            part = slice(s * feat, (s + 1) * feat)
            xr[pl.ds(hot_base(j, x, c), s1), part] = dot(selh[j * s1 : (j + 1) * s1], z2[:, part]).astype(BF16)
        hot_rings.append(
            Ring(
                nx,
                x,
                lambda i, j=j: rows(xr, hot_base(j, i, c), s1),
                lambda i, h, j=j: block(xr, hot_base(j, i, c), s1, h * (width // 2), width // 2),
                xdev,
                *pair(),
            )
        )
        siblings.append(([], *pair()))

    def to_sibling(j, i):
        items, send, recv = siblings[j]
        ref = rows(xr, hot_base(j, i, c), s1)
        item = pltpu.make_async_remote_copy(
            src_ref=ref,
            dst_ref=ref,
            send_sem=send.at[len(items)],
            recv_sem=recv.at[len(items)],
            device_id=pdev(x * CORES + 1 - c),
            device_id_type=MESH,
        )
        item.start()
        items.append(item)

    def hot_step(j):
        ring = hot_rings[j]
        k = ring.at
        ring.step()
        if k == 0:
            to_sibling(j, x)
        elif k < ring.steps:
            to_sibling(j, lax.rem(x + nx - k, nx))
            to_sibling(j, lax.rem(x + k, nx))
        else:
            to_sibling(j, lax.rem(x + k, nx))

    def hot_arrived(j):
        while hot_rings[j].at <= hot_rings[j].steps:
            hot_step(j)
        for item in siblings[j][0]:
            item.wait_recv()

    def front(i):
        part = pl.ds(i * chunk, chunk)
        acc[...] = jnp.zeros_like(acc)

        @pl.loop(0, ny)
        def _(q):
            features = pl.ds(pl.multiple_of(q * feat, feat), feat)
            a = xr[part, features]
            for half in range(2):
                acc[:, half * ff : (half + 1) * ff] += dot(a, wgu[half, features, :])

        gated = acc[:, 0:ff]
        value = gated / (1.0 + jnp.exp(-gated)) * acc[:, ff : 2 * ff]
        hid[part, pl.ds(pl.multiple_of(y * ff, ff), ff)] = value.astype(BF16)
        ref = block(hid, i * chunk, chunk, y * ff, ff)
        return go(Copies(ny, y, lambda m: ref, lambda m: block(hid, i * chunk, chunk, m * ff, ff), ydev, *pair()))

    def back(i, gathered):
        gathered.wait_recv()
        part = pl.ds(i * chunk, chunk)
        o[part, :] = dot(hid[part, :], wd[...]).astype(BF16)
        own = pl.ds(i * chunk + p * s1, s1)
        ro[own, :] = o[own, :]
        return go(
            Copies(
                npl,
                p,
                lambda m: rows(o, i * chunk + m * s1, s1),
                lambda m: rows(ro, i * chunk + m * s1, s1),
                pdev,
                *pair(),
            )
        )

    def back_hot(i, gathered):
        gathered.wait_recv()
        part = pl.ds(i * chunk, chunk)
        o[part, :] = jnp.where(own_hot, dot(hid[part, :], wd[...]), 0.0).astype(BF16)
        half = nx * s1
        away = rows(o, i * chunk + (1 - c) * half, half)
        item = pltpu.make_async_remote_copy(
            src_ref=away,
            dst_ref=rows(halves, (i - 2) * half, half),
            send_sem=half_send.at[i - 2],
            recv_sem=half_recv.at[i - 2],
            device_id=pdev(x * CORES + 1 - c),
            device_id_type=MESH,
        )
        item.start()
        siblings.append(([item], None, None))
        return item

    def back_chip(i, item):
        item.wait_recv()
        half = nx * s1
        kept = pl.ds(i * chunk + c * half, half)
        o[kept, :] += halves[pl.ds((i - 2) * half, half), :]
        own = pl.ds(i * chunk + x * s1, s1)
        ro[own, :] = o[pl.ds(i * chunk + c * half + x * s1, s1), :]
        return go(
            Copies(
                nx,
                x,
                lambda m: rows(o, i * chunk + c * half + m * s1, s1),
                lambda m: rows(ro, i * chunk + m * s1, s1),
                xdev,
                *pair(),
            )
        )

    def mixed(i, returned):
        returned.wait_recv()
        high = mixers[i].astype(BF16)
        low = (mixers[i] - high.astype(F32)).astype(BF16)
        used = nx * s1 if i > 1 else chunk
        both = jnp.concatenate([high[:, 0:used], low[:, 0:used]], axis=0)
        sums = dot(both, ro[pl.ds(i * chunk, used), :])
        return sums[0:cols] + sums[cols:]

    def block_for(b, ahead):
        return pl.ds(b * cols + lax.rem(z + ahead + nz, nz) * tok, tok)

    def slot(b, k):
        return pl.ds(b * cols + k * tok, tok)

    class Sums:
        def __init__(self, b):
            self.b = b
            self.sems = pair()
            self.items = []
            inbox[slot(b, 0), :] = mix[block_for(b, 0), :]
            whole, low, high = pl.ds(0, feat), pl.ds(0, feat // 2), pl.ds(feat // 2, feat // 2)
            if nz == 8:
                self.send(-1, -1, 1, whole)
                self.send(1, 1, 2, whole)
                self.send(-1, -3, 5, whole)
                self.send(1, 3, 6, whole)
                self.send(-2, -4, 7, low)
                self.send(2, 4, 7, high)
            else:
                for i in range(1, nz):
                    self.send(i, i, i, whole)

        def send(self, step, ahead, k, part):
            i = len(self.items)
            send, recv = self.sems
            item = pltpu.make_async_remote_copy(
                src_ref=mix.at[block_for(self.b, ahead), part],
                dst_ref=inbox.at[slot(self.b, k), part],
                send_sem=send.at[i],
                recv_sem=recv.at[i],
                device_id=zdev(lax.rem(z + step + nz, nz)),
                device_id_type=MESH,
            )
            item.start()
            self.items.append(item)

        def relay(self):
            if nz != 8:
                return
            for item in self.items[2:6]:
                item.wait_recv()
            b, half = self.b, feat // 2
            for ahead, k in ((-2, 5), (2, 6)):
                total = mix[block_for(b, ahead), :].astype(F32) + inbox[slot(b, k), :].astype(F32)
                opposite = inbox[slot(b, 7), :].astype(F32)
                nearer = iota((tok, feat), 1) < half if ahead < 0 else iota((tok, feat), 1) >= half
                mix[block_for(b, ahead), :] = (total + jnp.where(nearer, opposite, 0.0)).astype(BF16)
            whole = pl.ds(0, feat)
            self.send(-2, -2, 3, whole)
            self.send(2, 2, 4, whole)

        def finish(self):
            b = self.b
            if nz == 8:
                for item in self.items[:2] + self.items[6:]:
                    item.wait_recv()
            else:
                for item in self.items:
                    item.wait_recv()
            total = inbox[slot(b, 0), :].astype(F32)
            for k in range(1, 5 if nz == 8 else nz):
                total += inbox[slot(b, k), :].astype(F32)
            out[b * tok : (b + 1) * tok, :] = total

        def wait_send(self):
            for item in self.items:
                item.wait_send()

    half_send, half_recv = pair()
    hot_step(0)
    hot_step(1)
    x1.wait_recv()
    y1 = go(Copies(ny, y, lambda i: mine(rows(xr, 0, chunk)), lambda m: lanes(rows(xr, 0, chunk), m, feat), ydev, *pair()))

    hot_step(2)
    weights.wait()
    for copies in x2:
        copies.wait_recv()
    hot_step(0)
    h1 = front(1)
    hot_step(1)
    hot_arrived(0)
    h2 = front(2)
    hot_step(2)
    own_out.wait()
    out_y.wait_recv()
    r1 = back(1, h1)
    y1.wait_recv()
    h0 = front(0)
    hot_arrived(1)
    h3 = front(3)
    b2 = back_hot(2, h2)
    r0 = back(0, h0)
    r2 = back_chip(2, b2)
    hot_arrived(2)
    h4 = front(4)
    blend[...] = mixed(1, r1)
    b3 = back_hot(3, h3)
    mix[0:cols, :] = mixed(0, r0).astype(BF16)
    d1 = Sums(0)
    r3 = back_chip(3, b3)
    b4 = back_hot(4, h4)
    blend[...] += mixed(2, r2)
    r4 = back_chip(4, b4)
    blend[...] += mixed(3, r3)
    d1.relay()
    mix[cols : 2 * cols, :] = (blend[...] + mixed(4, r4)).astype(BF16)
    d2 = Sums(1)
    d2.relay()
    d1.finish()
    d2.finish()

    for copies in started + rings + hot_rings + [d1, d2]:
        copies.wait_send()
    for items, _, _ in siblings:
        for item in items:
            item.wait_send()


def shards(
    dims, tokens_one, experts_one, gates_one, tokens_two, experts_two, gates_two, replica_pick, home, w_gate_up, w_down
):
    nz, nx, ny = dims
    npl = nx * CORES
    tok, feat = tokens_one.shape
    width = feat * ny
    ff = w_gate_up.shape[3]
    cols = nz * tok
    chunk = npl * SLOT * nz
    chunks = 2 + COPIES
    vmem = pltpu.VMEM
    dma = pltpu.SemaphoreType.DMA
    size = max(nz, npl, ny, nx) + 4
    groups = 1 + 2 + ny + 2 + 1 + 1 + 2 + ny + 2 * COPIES + 1 + 1 + 2 * chunks + 2
    any_spec = pl.BlockSpec(memory_space=pl.ANY)
    in_vmem = pl.BlockSpec(memory_space=pltpu.VMEM)
    out = pl.pallas_call(
        functools.partial(kernel, dims),
        out_shape=jax.ShapeDtypeStruct((2 * tok, feat), F32),
        in_specs=[in_vmem] * 8 + [any_spec] * 2,
        out_specs=in_vmem,
        scratch_shapes=[
            vmem((128, 128), F32),
            vmem((cols, 128), F32),
            vmem((npl * 8, 128), F32),
            vmem((cols, feat), BF16),
            vmem((cols, width), BF16),
            vmem((chunk, feat), BF16),
            vmem((chunk, width), BF16),
            vmem((chunks * chunk, width), BF16),
            vmem((chunk, 2 * ff), F32),
            vmem((chunks * chunk, ff * ny), BF16),
            vmem((chunks * chunk, feat), BF16),
            vmem((chunks * chunk, feat), BF16),
            vmem((cols, feat), F32),
            vmem((2 * cols, feat), BF16),
            vmem((2 * cols, feat), BF16),
            vmem((COPIES * nx * SLOT * nz, feat), BF16),
            vmem(w_gate_up.shape[1:], BF16),
            vmem((ff * ny, feat), BF16),
            dma((2,)),
        ]
        + [dma((size,)) for _ in range(2 * groups)],
        compiler_params=pltpu.CompilerParams(
            collective_id=0, has_side_effects=True, vmem_limit_bytes=56 * 1024 * 1024
        ),
        cost_estimate=pl.CostEstimate(flops=10_000_000_000, bytes_accessed=16_000_000, transcendentals=0),
    )(
        tokens_one,
        tokens_two,
        experts_one.T,
        gates_one.T,
        experts_two.T,
        gates_two.T,
        replica_pick.T,
        home[None, :],
        w_gate_up,
        w_down,
    )
    return out[:tok].astype(BF16), out[tok:].astype(BF16)


def solution(mesh):
    placed = (
        P("expert", "inner"),
        P("expert", None),
        P("expert", None),
        P("expert", "inner"),
        P("expert", None),
        P("expert", None),
        P("expert", None),
        P(),
        P("expert", None, None, "inner"),
        P("expert", "inner", None),
    )
    experts, inner = mesh.shape["expert"], mesh.shape["inner"]
    nx = 4 if experts >= 16 else 2
    dims = (experts // (nx * CORES), nx, inner)
    return jax.shard_map(
        functools.partial(shards, dims),
        mesh=mesh,
        in_specs=placed,
        out_specs=(P("expert", "inner"), P("expert", "inner")),
        check_vma=False,
    )
```
